768 devices in a mesh: slab: 12 (over z), grp: 64 (over x, y, core).
Axes of the slice: x: 4, y: 8, z: 12, core: 2. Of those that a mesh axis runs over, the one named last changes fastest.
Arguments:
- coords: float32 [3, 6291456], P(None, ('slab', 'grp')), may hold values from -1 to 1
- charges: float32 [6291456], P(('slab', 'grp')), may hold values from -1.5 to 1.5
- multipoles: float32 [121, 393216], P(None, ('slab', 'grp')), may hold values from -6 to 6
- operators: float32 [8, 121, 121], replicated, may hold values from -0.5 to 0.5
- send_list: int32 [768, 1024], P(('slab', 'grp')), may hold values from 0 to 511
- near_list: int32 [393216, 8], P(('slab', 'grp')), may hold values from 0 to 1535
- m2l_source: int32 [768, 4096], P(('slab', 'grp')), may hold values from 0 to 1023
- m2l_target: int32 [768, 4096], P(('slab', 'grp')), may hold values from 0 to 512, as said below
- m2l_operator: int32 [768, 4096], P(('slab', 'grp')), may hold values from 0 to 7
Outputs:
- local_exp: float32 [121, 393216], P(None, ('slab', 'grp'))
- near_potential: float32 [6291456], P(('slab', 'grp'))
The draws below stay inside these ranges and needn't reach their ends.
Inputs may be any that keep to these rules, and one draw needn't show every extreme that they name: `m2l_target`: entries past a block's count of used slots hold 512, an empty slot; the first block uses all 4096 slots.
All inputs are finite; a program needn't handle non-finite values.
Results may differ from the reference program's by a relative error of at most 0.00011.
Values sent between devices are 32-bit elements; how exact they have to be, the bound alone decides.
A program may use at most 64 MiB of HBM per device.

```python
import jax
import jax.numpy as jnp
from jax import lax

NCOEF = 121
LEAF_PTS = 16
LEAVES_DEV = 512
NEAR = 8
CAP = 16
OPS = 8
LIST = 4096
TOTAL_LEAVES = 393216
POINTS = 6291456
N_SLAB = 12
N_GRP = 64


def draw_m2l_target(key, part):
    key = jax.random.fold_in(key, 7)
    count_key, leaf_key = jax.random.split(key)
    blocks_all = N_SLAB * N_GRP
    counts = jax.random.randint(count_key, (blocks_all, 1), LIST // 4, LIST + 1)
    counts = counts.at[0, 0].set(LIST)
    leaves = jax.random.randint(leaf_key, (blocks_all, LIST), 0, LEAVES_DEV)
    slots = jnp.arange(LIST, dtype=jnp.int32)[None, :]
    return jnp.where(slots < counts, leaves, LEAVES_DEV).astype(jnp.int32)


def plant(array, key, low, largest):
    longest = array.shape.index(max(array.shape))
    spots = []
    for shift in (0, 1):
        where = [jax.random.randint(jax.random.fold_in(key, axis), (), 0, length) for axis, length in enumerate(array.shape)]
        where[longest] = (where[longest] + shift) % array.shape[longest]
        spots.append(tuple(where))
    return array.at[spots[0]].set(low).at[spots[1]].set(largest)


def block_scale(stream_key, extent, cuts, smallest, high):
    factor_of = 1.0
    for position, blocks in cuts:
        heights = jax.random.uniform(jax.random.fold_in(jax.random.fold_in(stream_key, 6), position), (blocks,), jnp.float32, smallest / len(cuts), high / len(cuts))
        factor_of = factor_of * jnp.repeat(jnp.exp(heights), extent[position] // blocks).reshape((-1,) + (1,) * (len(extent) - 1 - position))
    return factor_of


def normal_values(rng, extent, width, reach, cuts=(), kind=jnp.bfloat16):
    entries = jax.random.normal(rng, extent, jnp.float32) * width
    if len(cuts) > 0:
        entries = block_scale(rng, extent, cuts, -0.22, 0.18) * entries
    return jnp.clip(entries, min=-reach, max=reach).astype(kind)


def setup_inputs(seed: int = 0) -> dict:
    key_list = jax.random.split(jax.random.key(seed), 10)
    coords = jnp.clip(jax.random.uniform(key_list[0], (3, POINTS), jnp.float32, -1.0, 1.0) * block_scale(key_list[0], (3, POINTS), ((1, 768),), -0.4, 0.0), -1.0, 1.0)
    charges = normal_values(key_list[1], (POINTS,), 0.1, 1.5, ((0, 768),), jnp.float32)
    multipoles = normal_values(key_list[2], (NCOEF, TOTAL_LEAVES), 1.0, 6.0, ((1, 768),), jnp.float32)
    operators = normal_values(key_list[3], (OPS, NCOEF, NCOEF), NCOEF ** -0.5, 0.5, (), jnp.float32)
    send_list = plant(jax.random.randint(key_list[4], (N_SLAB * N_GRP, N_GRP * CAP), 0, LEAVES_DEV), jax.random.fold_in(key_list[4], 1), 0, LEAVES_DEV - 1).astype(jnp.int32)
    near_list = plant(jax.random.randint(key_list[5], (TOTAL_LEAVES, NEAR), 0, 3 * LEAVES_DEV), jax.random.fold_in(key_list[5], 1), 0, (3 * LEAVES_DEV) - 1).astype(jnp.int32)
    m2l_source = plant(jax.random.randint(key_list[6], (N_SLAB * N_GRP, LIST), 0, N_GRP * CAP), jax.random.fold_in(key_list[6], 1), 0, (N_GRP * CAP) - 1).astype(jnp.int32)
    m2l_target = draw_m2l_target(jax.random.fold_in(key_list[9], 71), 0)
    m2l_operator = plant(jax.random.randint(key_list[8], (N_SLAB * N_GRP, LIST), 0, OPS), jax.random.fold_in(key_list[8], 1), 0, OPS - 1).astype(jnp.int32)
    return dict(coords=coords, charges=charges, multipoles=multipoles, operators=operators, send_list=send_list, near_list=near_list, m2l_source=m2l_source, m2l_target=m2l_target, m2l_operator=m2l_operator)


SOFT2 = 0.0625

def near_block(args):
    window, targets, lists = args
    picked = jnp.take(window, lists, axis=1)
    sources = picked.reshape(4, LEAVES_DEV, NEAR * LEAF_PTS)
    tgt = jnp.transpose(targets, (0, 2, 1))
    dx = tgt[0][:, :, None] - sources[0][None]
    dy = tgt[1][:, :, None] - sources[1][None]
    dz = tgt[2][:, :, None] - sources[2][None]
    inverse = 1.0 / jnp.sqrt(dx * dx + dy * dy + dz * dz + SOFT2)
    potential = lax.optimization_barrier(jnp.sum(inverse * sources[3][None], axis=2))
    return potential.T.reshape(-1)

def reference(coords, charges, multipoles, operators, send_list, near_list, m2l_source, m2l_target, m2l_operator):
    blocks_all = N_SLAB * N_GRP
    stacked = jnp.concatenate([coords, charges[None, :]], axis=0)
    blocks = stacked.reshape(4, N_SLAB, N_GRP, LEAVES_DEV, LEAF_PTS)
    padded = jnp.pad(blocks, ((0, 0), (1, 1), (0, 0), (0, 0), (0, 0)))
    window = jnp.concatenate([padded[:, :-2], padded[:, 1:-1], padded[:, 2:]], axis=3)
    window = jnp.transpose(window.reshape(4, blocks_all, 3 * LEAVES_DEV, LEAF_PTS), (1, 0, 2, 3))
    targets = jnp.transpose(blocks.reshape(4, blocks_all, LEAVES_DEV, LEAF_PTS), (1, 0, 2, 3))
    lists = near_list.reshape(blocks_all, LEAVES_DEV, NEAR)
    near_potential = lax.map(near_block, (window, targets, lists)).reshape(-1)
    sends = send_list.reshape(N_SLAB, N_GRP, N_GRP, CAP)
    base = (jnp.arange(N_SLAB, dtype=jnp.int32)[:, None] * N_GRP + jnp.arange(N_GRP, dtype=jnp.int32)[None, :]) * LEAVES_DEV
    global_index = sends + base[:, :, None, None]
    global_index = jnp.transpose(global_index, (0, 2, 1, 3)).reshape(blocks_all, N_GRP * CAP).astype(jnp.int32)

    def far_block(args):
        index_row, source_row, target_row, operator_row = args
        columns = jnp.take(multipoles, jnp.take(index_row, source_row), axis=1)
        matrices = jnp.take(operators, operator_row, axis=0)
        translated = jnp.einsum('ecd,de->ce', matrices, columns, precision=lax.Precision.HIGHEST)
        summed = jax.ops.segment_sum(translated.T, target_row, num_segments=LEAVES_DEV + 1)
        return summed[:LEAVES_DEV].T
    local_exp = lax.map(far_block, (global_index, m2l_source, m2l_target, m2l_operator))
    local_exp = jnp.transpose(local_exp, (1, 0, 2)).reshape(NCOEF, blocks_all * LEAVES_DEV)
    return (local_exp, near_potential)
```

```python
import jax
import jax.numpy as jnp
from jax import lax
from jax.experimental import pallas as pl
from jax.experimental.pallas import tpu as pltpu
from jax.sharding import PartitionSpec as P

SOFT2 = 0.0625
F32, BF16, I32 = jnp.float32, jnp.bfloat16, jnp.int32


def split(x):
    high = x.astype(BF16)
    return high, (x - high.astype(F32)).astype(BF16)


def send_rows(mult_ref, send_ref, held, out_ref):
    held[...] = jnp.zeros_like(held)
    held[0:121, :] = mult_ref[...]
    high, low = split(held[...])
    both = jnp.concatenate([high, low], axis=0)
    for k in range(4):
        cols = slice(256 * k, 256 * k + 256)
        pick = (lax.broadcasted_iota(I32, (512, 256), 0) == send_ref[:, cols]).astype(BF16)
        got = jnp.dot(both, pick, preferred_element_type=F32)
        out_ref[cols, :] = (got[:128] + got[128:]).T


def own_window(coords_ref, charges_ref, stage, own):
    for c in range(64):
        for q in range(3):
            stage[q // 2, pl.ds(64 * (q % 2) + c, 1), :] = coords_ref[q : q + 1, 128 * c : 128 * c + 128]
    stage[1, 64:128, :] = charges_ref[...]
    lane = lax.broadcasted_iota(I32, (16, 128), 1)
    for h in range(2):
        t = stage[h].T
        for j in range(4):
            left, right = t[32 * j : 32 * j + 16], t[32 * j + 16 : 32 * j + 32]
            own[j, 32 * h : 32 * h + 16, :] = jnp.where(lane < 64, left, pltpu.roll(right, 64, 1))
            own[j, 32 * h + 16 : 32 * h + 32, :] = jnp.where(lane < 64, pltpu.roll(left, 64, 1), right)


def take(x, index):
    return jnp.take_along_axis(x, index, axis=1)


def near_index(near_ref, tile_ref, lane_ref):
    lane = lax.broadcasted_iota(I32, (8, 128), 1)
    c, half = lane & 63, lane >> 6
    for j in range(4):
        spot = 8 * (c & 15) + 2 * j + half
        w = jnp.zeros((8, 128), I32)
        for k in range(4):
            w = jnp.where((c >> 4) == k, take(near_ref[:, 128 * k : 128 * k + 128], spot), w)
        leaf = w & 511
        tile_ref[j] = (w >> 9) * 4 + ((leaf & 7) >> 1)
        lane_ref[j] = (leaf & 1) * 64 + (leaf >> 3)


def near_gather(window, tile_ref, lane_ref, sources):
    def body(step, carry):
        j, n = step // 8, step % 8
        tile = jnp.broadcast_to(tile_ref[j, pl.ds(n, 1), :], (8, 128))
        spot = jnp.broadcast_to(lane_ref[j, pl.ds(n, 1), :], (8, 128))
        masks = [tile == k for k in range(12)]
        for r in range(8):
            rows = slice(8 * r, 8 * r + 8)
            got = take(window[0, rows, :], spot)
            for k in range(1, 12):
                got = jnp.where(masks[k], take(window[k, rows, :], spot), got)
            sources[j, n, rows, :] = got
        return carry

    lax.fori_loop(0, 32, body, 0)


def near_sum(own, sources, pot):
    def body(step, carry):
        j, i = step // 8, step % 8
        targets = [
            [jnp.broadcast_to(own[j, pl.ds(16 * q + i + 8 * u, 1), :], (8, 128)) for q in range(3)]
            for u in range(2)
        ]
        total = [jnp.zeros((8, 128), F32) for _ in range(2)]
        for n in range(8):
            for h in range(2):
                s = [sources[j, n, 16 * q + 8 * h : 16 * q + 8 * h + 8, :] for q in range(4)]
                for u in range(2):
                    dx, dy, dz = (targets[u][q] - s[q] for q in range(3))
                    total[u] = total[u] + s[3] * lax.rsqrt(dx * dx + dy * dy + dz * dz + SOFT2)
        for u in range(2):
            pot[j, pl.ds(i + 8 * u, 1), :] = jnp.sum(total[u], axis=0, keepdims=True)
        return carry

    lax.fori_loop(0, 32, body, 0)


def near_out(pot, flip, out_ref):
    for j in range(4):
        flip[32 * j : 32 * j + 16, :] = pot[j]
        flip[32 * j + 16 : 32 * j + 32, :] = pltpu.roll(pot[j], 64, 1)
    out_ref[...] = flip[...].T[0:64]


def operator_parts(ops_ref, pad, first, second):
    pad[...] = jnp.zeros_like(pad)
    for o in range(8):
        pad[0:121, 0:121] = ops_ref[:, o, :]
        high, low = split(pad[...])
        rows = slice(128 * (o % 2), 128 * (o % 2) + 128)
        first[o // 2, rows, 0:128] = high
        first[o // 2, rows, 128:256] = high
        second[o // 2, rows, :] = low


NT = (((1,), (1,)), ((), ()))


def translate(rows, first, second, table, start):
    count = rows.shape[0]
    high, low = split(rows)
    both = jnp.concatenate([high, low], axis=1)
    for k in range(4):
        got = lax.dot_general(both, first[k], NT, preferred_element_type=F32)
        got = got + lax.dot_general(high, second[k], NT, preferred_element_type=F32)
        table[pl.ds(2 * k * 1024 + start, count), :] = got[:, :128]
        table[pl.ds((2 * k + 1) * 1024 + start, count), :] = got[:, 128:]


def target_table(target_ref, hot):
    for k in range(16):
        cols = slice(256 * k, 256 * k + 256)
        hot[:, cols] = (lax.broadcasted_iota(I32, (512, 256), 0) == target_ref[:, cols]).astype(BF16)


def collect(index_ref, table, picked):
    def body(step, carry):
        base = step * 64
        for u in range(64):
            picked[pl.ds(base + u, 1), :] = table[pl.ds(index_ref[0, base + u], 1), :]
        return carry

    lax.fori_loop(0, 64, body, 0)


def gather_sum(hot, picked, total):
    total[...] = jnp.zeros_like(total)
    for k in range(8):
        rows = slice(512 * k, 512 * k + 512)
        high, low = split(picked[rows, :])
        both = jnp.concatenate([high, low], axis=1)
        total[...] += jnp.dot(hot[:, rows], both, preferred_element_type=F32)


def far_out(total, out_ref):
    for j in range(4):
        rows = slice(128 * j, 128 * j + 128)
        out_ref[:, rows] = (total[rows, :128] + total[rows, 128:]).T[0:121]


MESH = pl.DeviceIdType.MESH


def kernel(
    index_ref,
    coords_ref,
    charges_ref,
    mult_ref,
    ops_ref,
    send_ref,
    near_ref,
    target_ref,
    far_ref,
    pot_ref,
    stage,
    window,
    tile,
    spot,
    sources,
    pot,
    flip,
    held,
    outgoing,
    received,
    pad,
    first,
    second,
    table,
    hot,
    picked,
    total,
    halo_send,
    halo_recv,
    rows_send,
    rows_recv,
):
    slabs, groups = lax.axis_size("slab"), lax.axis_size("grp")
    s, g = lax.axis_index("slab"), lax.axis_index("grp")

    barrier = pltpu.get_barrier_semaphore()

    def greet(d, carry):
        other = lax.rem(g + d, groups)
        pl.semaphore_signal(barrier, inc=1, device_id={"grp": other}, device_id_type=MESH)
        return carry

    lax.fori_loop(1, groups, greet, 0)

    @pl.when(s > 0)
    def _():
        pl.semaphore_signal(barrier, inc=1, device_id={"slab": s - 1}, device_id_type=MESH)

    @pl.when(s < slabs - 1)
    def _():
        pl.semaphore_signal(barrier, inc=1, device_id={"slab": s + 1}, device_id_type=MESH)

    send_rows(mult_ref, send_ref, held, outgoing)
    own = window.at[4:8]
    own_window(coords_ref, charges_ref, stage, own)

    inner = jnp.where(s > 0, 1, 0) + jnp.where(s < slabs - 1, 1, 0)
    pl.semaphore_wait(barrier, groups - 1 + inner)

    def rows_copy(other):
        return pltpu.make_async_remote_copy(
            src_ref=outgoing.at[pl.ds(pl.multiple_of(16 * other, 16), 16)],
            dst_ref=received.at[pl.ds(pl.multiple_of(16 * g, 16), 16)],
            send_sem=rows_send,
            recv_sem=rows_recv.at[g // 8],
            device_id={"grp": other},
            device_id_type=MESH,
        )

    up = pltpu.make_async_remote_copy(
        src_ref=own,
        dst_ref=window.at[0:4],
        send_sem=halo_send.at[0],
        recv_sem=halo_recv.at[0],
        device_id={"slab": jnp.minimum(s + 1, slabs - 1)},
        device_id_type=MESH,
    )
    down = pltpu.make_async_remote_copy(
        src_ref=own,
        dst_ref=window.at[8:12],
        send_sem=halo_send.at[1],
        recv_sem=halo_recv.at[1],
        device_id={"slab": jnp.maximum(s - 1, 0)},
        device_id_type=MESH,
    )

    @pl.when(s < slabs - 1)
    def _():
        up.start()

    @pl.when(s > 0)
    def _():
        down.start()

    def send(d, carry):
        rows_copy(lax.rem(g + d, groups)).start()
        return carry

    lax.fori_loop(1, groups, send, 0)

    mine = pl.ds(pl.multiple_of(16 * g, 16), 16)
    received[mine, :] = outgoing[mine, :]

    near_index(near_ref, tile, spot)
    operator_parts(ops_ref, pad, first, second)
    target_table(target_ref, hot)

    @pl.when(s == 0)
    def _():
        window[0:4] = jnp.zeros((4, 64, 128), F32)

    @pl.when(s == slabs - 1)
    def _():
        window[8:12] = jnp.zeros((4, 64, 128), F32)

    @pl.when(s > 0)
    def _():
        up.wait_recv()

    @pl.when(s < slabs - 1)
    def _():
        down.wait_recv()

    near_gather(window, tile, spot, sources)
    near_sum(own, sources, pot)
    near_out(pot, flip, pot_ref)

    def arrived(count, k):
        block = pl.ds(0, 16 * count)
        return pltpu.make_async_remote_copy(
            src_ref=outgoing.at[block],
            dst_ref=received.at[block],
            send_sem=rows_send,
            recv_sem=rows_recv.at[k],
            device_id={"grp": lax.rem(g + 1, groups)},
            device_id_type=MESH,
        )

    for k in range(groups // 8):

        @pl.when(g // 8 == k)
        def _():
            arrived(7, k).wait_recv()

        @pl.when(g // 8 != k)
        def _():
            arrived(8, k).wait_recv()

        translate(received[128 * k : 128 * k + 128, :], first, second, table, 128 * k)

    collect(index_ref, table, picked)
    gather_sum(hot, picked, total)
    far_out(total, far_ref)

    arrived(groups - 1, 0).wait_send()

    @pl.when(s < slabs - 1)
    def _():
        up.wait_send()

    @pl.when(s > 0)
    def _():
        down.wait_send()


def shards(
    coords,
    charges,
    multipoles,
    operators,
    send_list,
    near_list,
    m2l_source,
    m2l_target,
    m2l_operator,
):
    index = m2l_operator * 1024 + m2l_source
    vmem = pl.BlockSpec(memory_space=pltpu.VMEM)
    far, pot = pl.pallas_call(
        kernel,
        out_shape=[jax.ShapeDtypeStruct((121, 512), F32), jax.ShapeDtypeStruct((64, 128), F32)],
        in_specs=[pl.BlockSpec(memory_space=pltpu.SMEM)] + [vmem] * 7,
        out_specs=[vmem, vmem],
        scratch_shapes=[
            pltpu.VMEM((2, 128, 128), F32),
            pltpu.VMEM((12, 64, 128), F32),
            pltpu.VMEM((4, 8, 128), I32),
            pltpu.VMEM((4, 8, 128), I32),
            pltpu.VMEM((4, 8, 64, 128), F32),
            pltpu.VMEM((4, 16, 128), F32),
            pltpu.VMEM((128, 128), F32),
            pltpu.VMEM((128, 512), F32),
            pltpu.VMEM((1024, 128), F32),
            pltpu.VMEM((1024, 128), F32),
            pltpu.VMEM((128, 128), F32),
            pltpu.VMEM((4, 256, 256), BF16),
            pltpu.VMEM((4, 256, 128), BF16),
            pltpu.VMEM((8192, 128), F32),
            pltpu.VMEM((512, 4096), BF16),
            pltpu.VMEM((4096, 128), F32),
            pltpu.VMEM((512, 256), F32),
            pltpu.SemaphoreType.DMA((2,)),
            pltpu.SemaphoreType.DMA((2,)),
            pltpu.SemaphoreType.DMA,
            pltpu.SemaphoreType.DMA((8,)),
        ],
        compiler_params=pltpu.CompilerParams(
            collective_id=0, has_side_effects=True, vmem_limit_bytes=40 * 2**20
        ),
    )(
        index,
        coords,
        charges.reshape(64, 128),
        multipoles,
        jnp.transpose(operators, (1, 0, 2)),
        send_list,
        near_list.T,
        m2l_target,
    )
    return far, pot.reshape(-1)


def solution(mesh):
    both = ("slab", "grp")
    return jax.shard_map(
        shards,
        mesh=mesh,
        in_specs=(P(None, both), P(both), P(None, both), P()) + (P(both, None),) * 5,
        out_specs=(P(None, both), P(both)),
        check_vma=False,
    )
```

```python
import jax
import jax.numpy as jnp
from jax import lax
from jax.experimental import pallas as pl
from jax.experimental.pallas import tpu as pltpu
from jax.sharding import PartitionSpec as P

SOFT2 = 0.0625
F32, BF16, I32 = jnp.float32, jnp.bfloat16, jnp.int32


def split(x):
    high = x.astype(BF16)
    return high, (x - high.astype(F32)).astype(BF16)


def send_rows(mult_ref, send_ref, held, out_ref):
    held[...] = jnp.zeros_like(held)
    held[0:121, :] = mult_ref[...]
    high, low = split(held[...])
    both = jnp.concatenate([high, low], axis=0)
    for k in range(4):
        cols = slice(256 * k, 256 * k + 256)
        pick = (lax.broadcasted_iota(I32, (512, 256), 0) == send_ref[:, cols]).astype(BF16)
        got = jnp.dot(both, pick, preferred_element_type=F32)
        out_ref[cols, :] = (got[:128] + got[128:]).T


def own_window(coords_ref, charges_ref, stage, own):
    for c in range(64):
        for q in range(3):
            stage[q // 2, pl.ds(64 * (q % 2) + c, 1), :] = coords_ref[q : q + 1, 128 * c : 128 * c + 128]
    stage[1, 64:128, :] = charges_ref[...]
    lane = lax.broadcasted_iota(I32, (16, 128), 1)
    for h in range(2):
        t = stage[h].T
        for j in range(4):
            left, right = t[32 * j : 32 * j + 16], t[32 * j + 16 : 32 * j + 32]
            own[j, 32 * h : 32 * h + 16, :] = jnp.where(lane < 64, left, pltpu.roll(right, 64, 1))
            own[j, 32 * h + 16 : 32 * h + 32, :] = jnp.where(lane < 64, pltpu.roll(left, 64, 1), right)


def take(x, index):
    return jnp.take_along_axis(x, index, axis=1)


def near_index(near_ref, tile_ref, lane_ref):
    lane = lax.broadcasted_iota(I32, (8, 128), 1)
    c, half = lane & 63, lane >> 6
    for j in range(4):
        spot = 8 * (c & 15) + 2 * j + half
        w = jnp.zeros((8, 128), I32)
        for k in range(4):
            w = jnp.where((c >> 4) == k, take(near_ref[:, 128 * k : 128 * k + 128], spot), w)
        leaf = w & 511
        tile_ref[j] = (w >> 9) * 4 + ((leaf & 7) >> 1)
        lane_ref[j] = (leaf & 1) * 64 + (leaf >> 3)


def near_hot(lane_ref, hots):
    spots = lax.broadcasted_iota(I32, (128, 128), 0)
    for step in range(16):
        j, n = step // 4, 2 * (step % 4)
        for u in range(2):
            hit = (spots == lane_ref[j, n + u : n + u + 1, :]).astype(BF16)
            hots[step, 0:128, 128 * u : 128 * u + 128] = hit
            hots[step, 128:256, 128 * u : 128 * u + 128] = hit


def near_table(window, cells, block):
    rows = slice(256 * block, 256 * block + 256)
    high, low = split(window[4 * block : 4 * block + 4].reshape(256, 128))
    cells[rows, 0:128] = high
    cells[rows, 128:256] = low


def near_gather(cells, tile_ref, hots, sources):
    def body(step, carry):
        j, n = step // 4, 2 * (step % 4)
        got = jnp.dot(cells[...], hots[step], preferred_element_type=F32)
        for u in range(2):
            tile = jnp.broadcast_to(tile_ref[j, pl.ds(n + u, 1), :], (8, 128))
            masks = [tile == k for k in range(1, 12)]
            cols = slice(128 * u, 128 * u + 128)
            for row in range(0, 64, 8):
                value = got[row : row + 8, cols]
                for k in range(1, 12):
                    value = jnp.where(masks[k - 1], got[64 * k + row : 64 * k + row + 8, cols], value)
                sources[j, n + u, row : row + 8, :] = value
        return carry

    lax.fori_loop(0, 16, body, 0)


def near_sum(own, sources, pot):
    def body(step, carry):
        j, i = step // 8, step % 8
        targets = [
            [jnp.broadcast_to(own[j, pl.ds(16 * q + i + 8 * u, 1), :], (8, 128)) for q in range(3)]
            for u in range(2)
        ]
        total = [jnp.zeros((8, 128), F32) for _ in range(2)]
        for n in range(8):
            for h in range(2):
                s = [sources[j, n, 16 * q + 8 * h : 16 * q + 8 * h + 8, :] for q in range(4)]
                for u in range(2):
                    dx, dy, dz = (targets[u][q] - s[q] for q in range(3))
                    total[u] = total[u] + s[3] * lax.rsqrt(dx * dx + dy * dy + dz * dz + SOFT2)
        for u in range(2):
            pot[j, pl.ds(i + 8 * u, 1), :] = jnp.sum(total[u], axis=0, keepdims=True)
        return carry

    lax.fori_loop(0, 32, body, 0)


def near_out(pot, flip, out_ref):
    for j in range(4):
        flip[32 * j : 32 * j + 16, :] = pot[j]
        flip[32 * j + 16 : 32 * j + 32, :] = pltpu.roll(pot[j], 64, 1)
    out_ref[...] = flip[...].T[0:64]


def operator_parts(ops_ref, pad, first, second):
    pad[...] = jnp.zeros_like(pad)
    for o in range(8):
        pad[0:121, 0:121] = ops_ref[:, o, :]
        high, low = split(pad[...])
        rows = slice(128 * (o % 2), 128 * (o % 2) + 128)
        first[o // 2, rows, 0:128] = high
        first[o // 2, rows, 128:256] = high
        second[o // 2, rows, :] = low


NT = (((1,), (1,)), ((), ()))


def translate(rows, first, second, table, start):
    count = rows.shape[0]
    high, low = split(rows)
    both = jnp.concatenate([high, low], axis=1)
    for k in range(4):
        got = lax.dot_general(both, first[k], NT, preferred_element_type=F32)
        got = got + lax.dot_general(high, second[k], NT, preferred_element_type=F32)
        table[pl.ds(2 * k * 1024 + start, count), :] = got[:, :128]
        table[pl.ds((2 * k + 1) * 1024 + start, count), :] = got[:, 128:]


def target_table(target_ref, hot):
    for k in range(16):
        cols = slice(256 * k, 256 * k + 256)
        hot[:, cols] = (lax.broadcasted_iota(I32, (512, 256), 0) == target_ref[:, cols]).astype(BF16)


def collect_sum(index_ref, table, hot, even, odd, total, size):
    chunks = 4096 // size

    def collect(base, picked):
        for u in range(size):
            picked[u : u + 1, :] = table[pl.ds(index_ref[0, base + u], 1), :]

    def add(base, picked):
        high, low = split(picked[...])
        both = jnp.concatenate([high, low], axis=1)
        cols = pl.ds(pl.multiple_of(base, size), size)
        total[...] += jnp.dot(hot[:, cols], both, preferred_element_type=F32)

    total[...] = jnp.zeros_like(total)
    collect(0, even)

    def body(step, carry):
        base = step * (2 * size)
        collect(base + size, odd)
        add(base, even)
        collect(base + 2 * size, even)
        add(base + size, odd)
        return carry

    lax.fori_loop(0, chunks // 2 - 1, body, 0)
    collect(4096 - size, odd)
    add(4096 - 2 * size, even)
    add(4096 - size, odd)


def far_out(total, out_ref):
    for j in range(4):
        rows = slice(128 * j, 128 * j + 128)
        out_ref[:, rows] = (total[rows, :128] + total[rows, 128:]).T[0:121]


MESH = pl.DeviceIdType.MESH
GROUPS = 64


def each_other(g, act):
    x, y, c = g // 16, (g // 2) % 8, g % 2

    def body(step, carry):
        i, r = step // 8, step % 8
        turn = (i + 1) // 2
        dy = jnp.where(i % 2 == 1, 4 - turn, 4 + turn)
        other = lax.rem(x + r // 2, 4) * 16 + lax.rem(y + dy, 8) * 2 + lax.rem(c + r % 2, 2)

        @pl.when((other != g) & (other != 0))
        def _():
            act(other)

        return carry

    lax.fori_loop(0, GROUPS, body, 0)


def kernel(
    coords_hbm,
    charges_hbm,
    mult_hbm,
    ops_hbm,
    send_hbm,
    near_hbm,
    source_hbm,
    target_hbm,
    kind_hbm,
    far_hbm,
    pot_hbm,
    coords,
    charges,
    mult,
    ops,
    sends,
    near,
    entry_source,
    entry_target,
    entry_kind,
    index_row,
    index,
    far_out_rows,
    pot_out_rows,
    stage,
    window,
    tile,
    spot,
    hots,
    cells,
    sources,
    pot,
    flip,
    held,
    outgoing,
    received,
    pad,
    first,
    second,
    table,
    hot,
    even,
    odd,
    total,
    load_sem,
    store_sem,
    halo_send,
    halo_recv,
    rows_send,
    rows_recv,
):
    slabs = lax.axis_size("slab")
    s, g = lax.axis_index("slab"), lax.axis_index("grp")
    barrier = pltpu.get_barrier_semaphore()

    def greet(other):
        pl.semaphore_signal(barrier, inc=1, device_id={"grp": other}, device_id_type=MESH)

    loads = [
        pltpu.make_async_copy(source, target, load_sem.at[i])
        for i, (source, target) in enumerate(
            [
                (mult_hbm, mult),
                (send_hbm, sends),
                (coords_hbm, coords),
                (charges_hbm, charges),
                (near_hbm, near),
                (ops_hbm, ops),
                (source_hbm, entry_source),
                (kind_hbm, entry_kind),
                (target_hbm, entry_target),
            ]
        )
    ]
    for load in loads:
        load.start()

    @pl.when(s > 0)
    def _():
        pl.semaphore_signal(barrier, inc=1, device_id={"slab": s - 1}, device_id_type=MESH)

    @pl.when(s < slabs - 1)
    def _():
        pl.semaphore_signal(barrier, inc=1, device_id={"slab": s + 1}, device_id_type=MESH)

    @pl.when(g != 0)
    def _():
        each_other(g, greet)

    loads[0].wait()
    loads[1].wait()
    send_rows(mult, sends, held, outgoing)
    loads[2].wait()
    loads[3].wait()
    own = window.at[4:8]
    own_window(coords, charges, stage, own)

    inner = jnp.where(s > 0, 1, 0) + jnp.where(s < slabs - 1, 1, 0)
    pl.semaphore_wait(barrier, GROUPS - 1 - jnp.where(g != 0, 1, 0) + inner)

    @pl.when(g != 0)
    def _():
        greet(0)

    up = pltpu.make_async_remote_copy(
        src_ref=own,
        dst_ref=window.at[0:4],
        send_sem=halo_send.at[0],
        recv_sem=halo_recv.at[0],
        device_id={"slab": jnp.minimum(s + 1, slabs - 1)},
        device_id_type=MESH,
    )
    down = pltpu.make_async_remote_copy(
        src_ref=own,
        dst_ref=window.at[8:12],
        send_sem=halo_send.at[1],
        recv_sem=halo_recv.at[1],
        device_id={"slab": jnp.maximum(s - 1, 0)},
        device_id_type=MESH,
    )

    @pl.when(s < slabs - 1)
    def _():
        up.start()

    @pl.when(s > 0)
    def _():
        down.start()

    @pl.when((g == 0) & (s > 0))
    def _():
        each_other(g, greet)

    def rows_copy(other):
        return pltpu.make_async_remote_copy(
            src_ref=outgoing.at[pl.ds(pl.multiple_of(16 * other, 16), 16)],
            dst_ref=received.at[pl.ds(pl.multiple_of(16 * g, 16), 16)],
            send_sem=rows_send,
            recv_sem=rows_recv.at[g // 16],
            device_id={"grp": other},
            device_id_type=MESH,
        )

    each_other(g, lambda other: rows_copy(other).start())

    @pl.when((g == 0) & (s == 0))
    def _():
        each_other(g, greet)

    mine = pl.ds(pl.multiple_of(16 * g, 16), 16)
    received[mine, :] = outgoing[mine, :]

    loads[4].wait()
    near_index(near, tile, spot)
    near_hot(spot, hots)
    loads[5].wait()
    operator_parts(ops, pad, first, second)
    loads[6].wait()
    loads[7].wait()
    index_row[...] = entry_kind[...] * 1024 + entry_source[...]
    index_load = pltpu.make_async_copy(index_row, index, load_sem.at[9])
    index_load.start()
    loads[8].wait()
    target_table(entry_target, hot)
    near_table(window, cells, 1)

    @pl.when(s == 0)
    def _():
        window[0:4] = jnp.zeros((4, 64, 128), F32)

    @pl.when(s == slabs - 1)
    def _():
        window[8:12] = jnp.zeros((4, 64, 128), F32)

    @pl.when(s > 0)
    def _():
        up.wait_recv()

    @pl.when(s < slabs - 1)
    def _():
        down.wait_recv()

    near_table(window, cells, 0)
    near_table(window, cells, 2)
    near_gather(cells, tile, hots, sources)

    @pl.when(g != 0)
    def _():
        pl.semaphore_wait(barrier, 1)
        rows_copy(0).start()

    near_sum(own, sources, pot)
    near_out(pot, flip, pot_out_rows)
    pot_store = pltpu.make_async_copy(pot_out_rows, pot_hbm, store_sem.at[0])
    pot_store.start()
    index_load.wait()

    def arrived(count, k):
        block = pl.ds(0, 16 * count)
        return pltpu.make_async_remote_copy(
            src_ref=outgoing.at[block],
            dst_ref=received.at[block],
            send_sem=rows_send,
            recv_sem=rows_recv.at[k],
            device_id={"grp": lax.rem(g + 1, GROUPS)},
            device_id_type=MESH,
        )

    for turn in (0, 1, 3, 2):
        k = lax.rem(g // 16 + turn, 4)
        arrived(15 if turn == 0 else 16, k).wait_recv()
        start = pl.multiple_of(256 * k, 256)
        translate(received[pl.ds(start, 256), :], first, second, table, start)

    collect_sum(index, table, hot, even, odd, total, 512)
    far_out(total, far_out_rows)
    far_store = pltpu.make_async_copy(far_out_rows, far_hbm, store_sem.at[1])
    far_store.start()

    arrived(GROUPS - 1, 0).wait_send()

    @pl.when(s < slabs - 1)
    def _():
        up.wait_send()

    @pl.when(s > 0)
    def _():
        down.wait_send()

    pot_store.wait()
    far_store.wait()


def shards(
    coords,
    charges,
    multipoles,
    operators,
    send_list,
    near_list,
    m2l_source,
    m2l_target,
    m2l_operator,
):
    hbm = pl.BlockSpec(memory_space=pltpu.HBM)
    vmem, dma = pltpu.VMEM, pltpu.SemaphoreType.DMA
    far, pot = pl.pallas_call(
        kernel,
        out_shape=[jax.ShapeDtypeStruct((121, 512), F32), jax.ShapeDtypeStruct((64, 128), F32)],
        in_specs=[hbm] * 9,
        out_specs=[hbm] * 2,
        scratch_shapes=[
            vmem((3, 8192), F32),
            vmem((64, 128), F32),
            vmem((121, 512), F32),
            vmem((121, 8, 121), F32),
            vmem((1, 1024), I32),
            vmem((8, 512), I32),
            vmem((1, 4096), I32),
            vmem((1, 4096), I32),
            vmem((1, 4096), I32),
            vmem((1, 4096), I32),
            pltpu.SMEM((1, 4096), I32),
            vmem((121, 512), F32),
            vmem((64, 128), F32),
            vmem((2, 128, 128), F32),
            vmem((12, 64, 128), F32),
            vmem((4, 8, 128), I32),
            vmem((4, 8, 128), I32),
            vmem((16, 256, 256), BF16),
            vmem((768, 256), BF16),
            vmem((4, 8, 64, 128), F32),
            vmem((4, 16, 128), F32),
            vmem((128, 128), F32),
            vmem((128, 512), F32),
            vmem((1024, 128), F32),
            vmem((1024, 128), F32),
            vmem((128, 128), F32),
            vmem((4, 256, 256), BF16),
            vmem((4, 256, 128), BF16),
            vmem((8192, 128), F32),
            vmem((512, 4096), BF16),
            vmem((512, 128), F32),
            vmem((512, 128), F32),
            vmem((512, 256), F32),
            dma((10,)),
            dma((2,)),
            dma((2,)),
            dma((2,)),
            dma,
            dma((4,)),
        ],
        compiler_params=pltpu.CompilerParams(
            collective_id=0, has_side_effects=True, vmem_limit_bytes=60 * 2**20
        ),
    )(
        coords,
        charges.reshape(64, 128),
        multipoles,
        jnp.transpose(operators, (1, 0, 2)),
        send_list,
        near_list.T,
        m2l_source,
        m2l_target,
        m2l_operator,
    )
    return far, pot.reshape(-1)


def solution(mesh):
    both = ("slab", "grp")
    return jax.shard_map(
        shards,
        mesh=mesh,
        in_specs=(P(None, both), P(both), P(None, both), P()) + (P(both, None),) * 5,
        out_specs=(P(None, both), P(both)),
        check_vma=False,
    )
```

```python
import jax
import jax.numpy as jnp
from jax import lax
from jax.experimental import pallas as pl
from jax.experimental.pallas import tpu as pltpu
from jax.sharding import PartitionSpec as P

SOFT2 = 0.0625
F32, BF16, I32 = jnp.float32, jnp.bfloat16, jnp.int32


def split(x):
    high = x.astype(BF16)
    return high, (x - high.astype(F32)).astype(BF16)


def send_rows(mult_ref, send_ref, held, out_ref):
    held[...] = jnp.zeros_like(held)
    held[0:121, :] = mult_ref[...]
    high, low = split(held[...])
    both = jnp.concatenate([high, low], axis=0)
    for k in range(4):
        cols = slice(256 * k, 256 * k + 256)
        pick = (lax.broadcasted_iota(I32, (512, 256), 0) == send_ref[:, cols]).astype(BF16)
        got = jnp.dot(both, pick, preferred_element_type=F32)
        out_ref[cols, :] = (got[:128] + got[128:]).T


def own_window(coords_ref, charges_ref, stage, own):
    for c in range(64):
        for q in range(3):
            stage[q // 2, pl.ds(64 * (q % 2) + c, 1), :] = coords_ref[q : q + 1, 128 * c : 128 * c + 128]
    stage[1, 64:128, :] = charges_ref[...]
    lane = lax.broadcasted_iota(I32, (16, 128), 1)
    for h in range(2):
        t = stage[h].T
        for j in range(4):
            left, right = t[32 * j : 32 * j + 16], t[32 * j + 16 : 32 * j + 32]
            own[j, 32 * h : 32 * h + 16, :] = jnp.where(lane < 64, left, pltpu.roll(right, 64, 1))
            own[j, 32 * h + 16 : 32 * h + 32, :] = jnp.where(lane < 64, pltpu.roll(left, 64, 1), right)


def take(x, index):
    return jnp.take_along_axis(x, index, axis=1)


def near_index(near_ref, tile_ref, lane_ref):
    lane = lax.broadcasted_iota(I32, (8, 128), 1)
    c, half = lane & 63, lane >> 6
    for j in range(4):
        spot = 8 * (c & 15) + 2 * j + half
        w = jnp.zeros((8, 128), I32)
        for k in range(4):
            w = jnp.where((c >> 4) == k, take(near_ref[:, 128 * k : 128 * k + 128], spot), w)
        leaf = w & 511
        tile_ref[j] = (w >> 9) * 4 + ((leaf & 7) >> 1)
        lane_ref[j] = (leaf & 1) * 64 + (leaf >> 3)


def near_hot(lane_ref, hots):
    spots = lax.broadcasted_iota(I32, (128, 128), 0)
    for step in range(16):
        j, n = step // 4, 2 * (step % 4)
        for u in range(2):
            hit = (spots == lane_ref[j, n + u : n + u + 1, :]).astype(BF16)
            hots[step, 0:128, 128 * u : 128 * u + 128] = hit
            hots[step, 128:256, 128 * u : 128 * u + 128] = hit


def near_table(window, cells, block):
    rows = slice(256 * block, 256 * block + 256)
    high, low = split(window[4 * block : 4 * block + 4].reshape(256, 128))
    cells[rows, 0:128] = high
    cells[rows, 128:256] = low


def near_gather(cells, tile_ref, hots, sources):
    def body(step, carry):
        j, n = step // 4, 2 * (step % 4)
        got = jnp.dot(cells[...], hots[step], preferred_element_type=F32)
        for u in range(2):
            tile = jnp.broadcast_to(tile_ref[j, pl.ds(n + u, 1), :], (8, 128))
            masks = [tile == k for k in range(1, 12)]
            cols = slice(128 * u, 128 * u + 128)
            for row in range(0, 64, 8):
                value = got[row : row + 8, cols]
                for k in range(1, 12):
                    value = jnp.where(masks[k - 1], got[64 * k + row : 64 * k + row + 8, cols], value)
                sources[j, n + u, row : row + 8, :] = value
        return carry

    lax.fori_loop(0, 16, body, 0)


def near_sum(own, sources, pot):
    def body(step, carry):
        j, i = step // 8, step % 8
        targets = [
            [jnp.broadcast_to(own[j, pl.ds(16 * q + i + 8 * u, 1), :], (8, 128)) for q in range(3)]
            for u in range(2)
        ]
        total = [jnp.zeros((8, 128), F32) for _ in range(2)]
        for n in range(8):
            for h in range(2):
                s = [sources[j, n, 16 * q + 8 * h : 16 * q + 8 * h + 8, :] for q in range(4)]
                for u in range(2):
                    dx, dy, dz = (targets[u][q] - s[q] for q in range(3))
                    total[u] = total[u] + s[3] * lax.rsqrt(dx * dx + dy * dy + dz * dz + SOFT2)
        for u in range(2):
            pot[j, pl.ds(i + 8 * u, 1), :] = jnp.sum(total[u], axis=0, keepdims=True)
        return carry

    lax.fori_loop(0, 32, body, 0)


def near_out(pot, flip, out_ref):
    for j in range(4):
        flip[32 * j : 32 * j + 16, :] = pot[j]
        flip[32 * j + 16 : 32 * j + 32, :] = pltpu.roll(pot[j], 64, 1)
    out_ref[...] = flip[...].T[0:64]


def operator_parts(ops_ref, pad, first, second):
    pad[...] = jnp.zeros_like(pad)
    for o in range(8):
        pad[0:121, 0:121] = ops_ref[:, o, :]
        high, low = split(pad[...])
        rows = slice(128 * (o % 2), 128 * (o % 2) + 128)
        first[o // 2, rows, 0:128] = high
        first[o // 2, rows, 128:256] = high
        second[o // 2, rows, :] = low


NT = (((1,), (1,)), ((), ()))


def translate(rows, first, second, table, start):
    count = rows.shape[0]
    high, low = split(rows)
    both = jnp.concatenate([high, low], axis=1)
    for k in range(4):
        got = lax.dot_general(both, first[k], NT, preferred_element_type=F32)
        got = got + lax.dot_general(high, second[k], NT, preferred_element_type=F32)
        table[pl.ds(2 * k * 1024 + start, count), :] = got[:, :128]
        table[pl.ds((2 * k + 1) * 1024 + start, count), :] = got[:, 128:]


def target_table(target_ref, hot):
    for k in range(16):
        cols = slice(256 * k, 256 * k + 256)
        hot[:, cols] = (lax.broadcasted_iota(I32, (512, 256), 0) == target_ref[:, cols]).astype(BF16)


def collect_sum(index_ref, table, hot, even, odd, total, size):
    chunks = 4096 // size

    def collect(base, picked):
        for u in range(size):
            picked[u : u + 1, :] = table[pl.ds(index_ref[0, base + u], 1), :]

    def add(base, picked):
        high, low = split(picked[...])
        both = jnp.concatenate([high, low], axis=1)
        cols = pl.ds(pl.multiple_of(base, size), size)
        total[...] += jnp.dot(hot[:, cols], both, preferred_element_type=F32)

    total[...] = jnp.zeros_like(total)
    collect(0, even)

    def body(step, carry):
        base = step * (2 * size)
        collect(base + size, odd)
        add(base, even)
        collect(base + 2 * size, even)
        add(base + size, odd)
        return carry

    lax.fori_loop(0, chunks // 2 - 1, body, 0)
    collect(4096 - size, odd)
    add(4096 - 2 * size, even)
    add(4096 - size, odd)


def far_out(total, out_ref):
    for j in range(4):
        rows = slice(128 * j, 128 * j + 128)
        out_ref[:, rows] = (total[rows, :128] + total[rows, 128:]).T[0:121]


MESH = pl.DeviceIdType.MESH
GROUPS = 64


def each_other(g, skip, act):
    x, y, c = g // 16, (g // 2) % 8, g % 2

    def body(step, carry):
        i, r = step // 8, step % 8
        turn = (i + 1) // 2
        dy = jnp.where(i % 2 == 1, 4 - turn, 4 + turn)
        other = lax.rem(x + r // 2, 4) * 16 + lax.rem(y + dy, 8) * 2 + lax.rem(c + r % 2, 2)

        @pl.when((other != g) & (other != skip))
        def _():
            act(other)

        return carry

    lax.fori_loop(0, GROUPS, body, 0)


def kernel(
    coords_hbm,
    charges_hbm,
    mult_hbm,
    ops_hbm,
    send_hbm,
    near_hbm,
    source_hbm,
    target_hbm,
    kind_hbm,
    far_rows,
    pot_rows,
    coords,
    charges,
    mult,
    ops,
    sends,
    near,
    entry_source,
    entry_target,
    entry_kind,
    index_row,
    index,
    stage,
    window,
    tile,
    spot,
    hots,
    cells,
    sources,
    pot,
    flip,
    held,
    outgoing,
    received,
    pad,
    first,
    second,
    table,
    hot,
    even,
    odd,
    total,
    load_sem,
    halo_send,
    halo_recv,
    rows_send,
    rows_recv,
):
    slabs = lax.axis_size("slab")
    s, g = lax.axis_index("slab"), lax.axis_index("grp")
    barrier = pltpu.get_barrier_semaphore()

    def greet(other):
        pl.semaphore_signal(barrier, inc=1, device_id={"grp": other}, device_id_type=MESH)

    loads = [
        pltpu.make_async_copy(source, target, load_sem.at[i])
        for i, (source, target) in enumerate(
            [
                (mult_hbm, mult),
                (send_hbm, sends),
                (coords_hbm, coords),
                (charges_hbm, charges),
                (near_hbm, near),
                (ops_hbm, ops),
                (source_hbm, entry_source),
                (kind_hbm, entry_kind),
                (target_hbm, entry_target),
            ]
        )
    ]
    for load in loads:
        load.start()

    @pl.when(s > 0)
    def _():
        pl.semaphore_signal(barrier, inc=1, device_id={"slab": s - 1}, device_id_type=MESH)

    @pl.when(s < slabs - 1)
    def _():
        pl.semaphore_signal(barrier, inc=1, device_id={"slab": s + 1}, device_id_type=MESH)

    late = (s == 0) & (g == 0)
    meets_late = (s == 0) & (g != 0)
    skip = jnp.where(s == 0, 0, GROUPS)

    @pl.when(jnp.logical_not(late))
    def _():
        each_other(g, skip, greet)

    loads[0].wait()
    loads[1].wait()
    send_rows(mult, sends, held, outgoing)
    loads[2].wait()
    loads[3].wait()
    own = window.at[4:8]
    own_window(coords, charges, stage, own)

    inner = jnp.where(s > 0, 1, 0) + jnp.where(s < slabs - 1, 1, 0)
    pl.semaphore_wait(barrier, GROUPS - 1 - jnp.where(meets_late, 1, 0) + inner)

    @pl.when(meets_late)
    def _():
        greet(0)

    up = pltpu.make_async_remote_copy(
        src_ref=own,
        dst_ref=window.at[0:4],
        send_sem=halo_send.at[0],
        recv_sem=halo_recv.at[0],
        device_id={"slab": jnp.minimum(s + 1, slabs - 1)},
        device_id_type=MESH,
    )
    down = pltpu.make_async_remote_copy(
        src_ref=own,
        dst_ref=window.at[8:12],
        send_sem=halo_send.at[1],
        recv_sem=halo_recv.at[1],
        device_id={"slab": jnp.maximum(s - 1, 0)},
        device_id_type=MESH,
    )

    @pl.when(s < slabs - 1)
    def _():
        up.start()

    @pl.when(s > 0)
    def _():
        down.start()

    def rows_copy(other):
        return pltpu.make_async_remote_copy(
            src_ref=outgoing.at[pl.ds(pl.multiple_of(16 * other, 16), 16)],
            dst_ref=received.at[pl.ds(pl.multiple_of(16 * g, 16), 16)],
            send_sem=rows_send,
            recv_sem=rows_recv.at[g // 16],
            device_id={"grp": other},
            device_id_type=MESH,
        )

    each_other(g, skip, lambda other: rows_copy(other).start())

    @pl.when(late)
    def _():
        each_other(g, skip, greet)

    mine = pl.ds(pl.multiple_of(16 * g, 16), 16)
    received[mine, :] = outgoing[mine, :]

    loads[4].wait()
    near_index(near, tile, spot)
    near_hot(spot, hots)
    loads[5].wait()
    operator_parts(ops, pad, first, second)
    loads[6].wait()
    loads[7].wait()
    index_row[...] = entry_kind[...] * 1024 + entry_source[...]
    index_load = pltpu.make_async_copy(index_row, index, load_sem.at[9])
    index_load.start()
    loads[8].wait()
    target_table(entry_target, hot)
    near_table(window, cells, 1)

    @pl.when(s == 0)
    def _():
        window[0:4] = jnp.zeros((4, 64, 128), F32)

    @pl.when(s == slabs - 1)
    def _():
        window[8:12] = jnp.zeros((4, 64, 128), F32)

    @pl.when(s > 0)
    def _():
        up.wait_recv()

    @pl.when(s < slabs - 1)
    def _():
        down.wait_recv()

    near_table(window, cells, 0)
    near_table(window, cells, 2)
    near_gather(cells, tile, hots, sources)

    near_sum(own, sources, pot)
    near_out(pot, flip, pot_rows)
    index_load.wait()

    def arrived(count, k):
        block = pl.ds(0, 16 * count)
        return pltpu.make_async_remote_copy(
            src_ref=outgoing.at[block],
            dst_ref=received.at[block],
            send_sem=rows_send,
            recv_sem=rows_recv.at[k],
            device_id={"grp": lax.rem(g + 1, GROUPS)},
            device_id_type=MESH,
        )

    for k in (1, 2, 3, 0):
        if k == 0:

            @pl.when(meets_late)
            def _():
                pl.semaphore_wait(barrier, 1)
                rows_copy(0).start()

        @pl.when(g // 16 == k)
        def _():
            arrived(15, k).wait_recv()

        @pl.when(g // 16 != k)
        def _():
            arrived(16, k).wait_recv()

        translate(received[256 * k : 256 * k + 256, :], first, second, table, 256 * k)

    collect_sum(index, table, hot, even, odd, total, 512)
    far_out(total, far_rows)

    arrived(GROUPS - 1, 0).wait_send()

    @pl.when(s < slabs - 1)
    def _():
        up.wait_send()

    @pl.when(s > 0)
    def _():
        down.wait_send()


def shards(
    coords,
    charges,
    multipoles,
    operators,
    send_list,
    near_list,
    m2l_source,
    m2l_target,
    m2l_operator,
):
    operands = (
        coords,
        charges.reshape(64, 128),
        multipoles,
        jnp.transpose(operators, (1, 0, 2)),
        send_list,
        near_list.T,
        m2l_source,
        m2l_target,
        m2l_operator,
    )
    hbm = pl.BlockSpec(memory_space=pltpu.HBM)
    vmem, dma = pltpu.VMEM, pltpu.SemaphoreType.DMA
    far, pot = pl.pallas_call(
        kernel,
        out_shape=[vmem((121, 512), F32), vmem((64, 128), F32)],
        in_specs=[hbm] * 9,
        out_specs=[pl.BlockSpec(memory_space=vmem)] * 2,
        scratch_shapes=[
            vmem((3, 8192), F32),
            vmem((64, 128), F32),
            vmem((121, 512), F32),
            vmem((121, 8, 121), F32),
            vmem((1, 1024), I32),
            vmem((8, 512), I32),
            vmem((1, 4096), I32),
            vmem((1, 4096), I32),
            vmem((1, 4096), I32),
            vmem((1, 4096), I32),
            pltpu.SMEM((1, 4096), I32),
            vmem((2, 128, 128), F32),
            vmem((12, 64, 128), F32),
            vmem((4, 8, 128), I32),
            vmem((4, 8, 128), I32),
            vmem((16, 256, 256), BF16),
            vmem((768, 256), BF16),
            vmem((4, 8, 64, 128), F32),
            vmem((4, 16, 128), F32),
            vmem((128, 128), F32),
            vmem((128, 512), F32),
            vmem((1024, 128), F32),
            vmem((1024, 128), F32),
            vmem((128, 128), F32),
            vmem((4, 256, 256), BF16),
            vmem((4, 256, 128), BF16),
            vmem((8192, 128), F32),
            vmem((512, 4096), BF16),
            vmem((512, 128), F32),
            vmem((512, 128), F32),
            vmem((512, 256), F32),
            dma((10,)),
            dma((2,)),
            dma((2,)),
            dma,
            dma((4,)),
        ],
        compiler_params=pltpu.CompilerParams(
            collective_id=0, has_side_effects=True, vmem_limit_bytes=48 * 2**20
        ),
    )(*(pltpu.with_memory_space_constraint(x, pltpu.HBM) for x in operands))
    return far, pot.reshape(-1)


def solution(mesh):
    both = ("slab", "grp")
    return jax.shard_map(
        shards,
        mesh=mesh,
        in_specs=(P(None, both), P(both), P(None, both), P()) + (P(both, None),) * 5,
        out_specs=(P(None, both), P(both)),
        check_vma=False,
    )
```

```python
import functools
import jax
import jax.numpy as jnp
from jax import lax
from jax.experimental import pallas as pl
from jax.experimental.pallas import tpu as pltpu
from jax.sharding import PartitionSpec as P

SOFT2 = 0.0625
F32, BF16, I32 = jnp.float32, jnp.bfloat16, jnp.int32


def split(x):
    high = x.astype(BF16)
    return high, (x - high.astype(F32)).astype(BF16)


def send_rows(mult_ref, send_ref, held, out_ref):
    held[...] = jnp.zeros_like(held)
    held[0:121, :] = mult_ref[...]
    high, low = split(held[...])
    both = jnp.concatenate([high, low], axis=0)
    for k in range(4):
        cols = slice(256 * k, 256 * k + 256)
        pick = (lax.broadcasted_iota(I32, (512, 256), 0) == send_ref[:, cols]).astype(BF16)
        got = jnp.dot(both, pick, preferred_element_type=F32)
        out_ref[cols, :] = (got[:128] + got[128:]).T


def own_window(coords_ref, charges_ref, stage, own):
    for c in range(64):
        for q in range(3):
            stage[q // 2, pl.ds(64 * (q % 2) + c, 1), :] = coords_ref[q : q + 1, 128 * c : 128 * c + 128]
    stage[1, 64:128, :] = charges_ref[...]
    lane = lax.broadcasted_iota(I32, (16, 128), 1)
    for h in range(2):
        t = stage[h].T
        for j in range(4):
            left, right = t[32 * j : 32 * j + 16], t[32 * j + 16 : 32 * j + 32]
            own[j, 32 * h : 32 * h + 16, :] = jnp.where(lane < 64, left, pltpu.roll(right, 64, 1))
            own[j, 32 * h + 16 : 32 * h + 32, :] = jnp.where(lane < 64, pltpu.roll(left, 64, 1), right)


def take(x, index):
    return jnp.take_along_axis(x, index, axis=1)


def near_index(near_ref, tile_ref, lane_ref):
    lane = lax.broadcasted_iota(I32, (8, 128), 1)
    c, half = lane & 63, lane >> 6
    for j in range(4):
        spot = 8 * (c & 15) + 2 * j + half
        w = jnp.zeros((8, 128), I32)
        for k in range(4):
            w = jnp.where((c >> 4) == k, take(near_ref[:, 128 * k : 128 * k + 128], spot), w)
        leaf = w & 511
        tile_ref[j] = (w >> 9) * 4 + ((leaf & 7) >> 1)
        lane_ref[j] = (leaf & 1) * 64 + (leaf >> 3)


def near_hot(lane_ref, hots):
    spots = lax.broadcasted_iota(I32, (128, 128), 0)
    for step in range(16):
        j, n = step // 4, 2 * (step % 4)
        for u in range(2):
            hit = (spots == lane_ref[j, n + u : n + u + 1, :]).astype(BF16)
            hots[step, 0:128, 128 * u : 128 * u + 128] = hit
            hots[step, 128:256, 128 * u : 128 * u + 128] = hit


def near_table(window, cells, block):
    rows = slice(256 * block, 256 * block + 256)
    high, low = split(window[4 * block : 4 * block + 4].reshape(256, 128))
    cells[rows, 0:128] = high
    cells[rows, 128:256] = low


def near_gather(cells, tile_ref, hots, sources):
    def body(step, carry):
        j, n = step // 4, 2 * (step % 4)
        got = jnp.dot(cells[...], hots[step], preferred_element_type=F32)
        for u in range(2):
            tile = jnp.broadcast_to(tile_ref[j, pl.ds(n + u, 1), :], (8, 128))
            masks = [tile == k for k in range(1, 12)]
            cols = slice(128 * u, 128 * u + 128)
            for row in range(0, 64, 8):
                value = got[row : row + 8, cols]
                for k in range(1, 12):
                    value = jnp.where(masks[k - 1], got[64 * k + row : 64 * k + row + 8, cols], value)
                sources[j, n + u, row : row + 8, :] = value
        return carry

    lax.fori_loop(0, 16, body, 0)


def near_sum(own, sources, pot):
    def body(step, carry):
        j, i = step // 8, step % 8
        targets = [
            [jnp.broadcast_to(own[j, pl.ds(16 * q + i + 8 * u, 1), :], (8, 128)) for q in range(3)]
            for u in range(2)
        ]
        total = [jnp.zeros((8, 128), F32) for _ in range(2)]
        for n in range(8):
            for h in range(2):
                s = [sources[j, n, 16 * q + 8 * h : 16 * q + 8 * h + 8, :] for q in range(4)]
                for u in range(2):
                    dx, dy, dz = (targets[u][q] - s[q] for q in range(3))
                    total[u] = total[u] + s[3] * lax.rsqrt(dx * dx + dy * dy + dz * dz + SOFT2)
        for u in range(2):
            pot[j, pl.ds(i + 8 * u, 1), :] = jnp.sum(total[u], axis=0, keepdims=True)
        return carry

    lax.fori_loop(0, 32, body, 0)


def near_out(pot, flip, out_ref):
    for j in range(4):
        flip[32 * j : 32 * j + 16, :] = pot[j]
        flip[32 * j + 16 : 32 * j + 32, :] = pltpu.roll(pot[j], 64, 1)
    out_ref[...] = flip[...].T[0:64]


def operator_parts(ops_ref, pad, first, second):
    pad[...] = jnp.zeros_like(pad)
    for o in range(8):
        pad[0:121, 0:121] = ops_ref[:, o, :]
        high, low = split(pad[...])
        rows = slice(128 * (o % 2), 128 * (o % 2) + 128)
        first[o // 2, rows, 0:128] = high
        first[o // 2, rows, 128:256] = high
        second[o // 2, rows, :] = low


NT = (((1,), (1,)), ((), ()))


def translate(rows, first, second, table, start):
    count = rows.shape[0]
    high, low = split(rows)
    both = jnp.concatenate([high, low], axis=1)
    for k in range(4):
        got = lax.dot_general(both, first[k], NT, preferred_element_type=F32)
        got = got + lax.dot_general(high, second[k], NT, preferred_element_type=F32)
        table[pl.ds(2 * k * 1024 + start, count), :] = got[:, :128]
        table[pl.ds((2 * k + 1) * 1024 + start, count), :] = got[:, 128:]


def target_table(target_ref, hot):
    for k in range(16):
        cols = slice(256 * k, 256 * k + 256)
        hot[:, cols] = (lax.broadcasted_iota(I32, (512, 256), 0) == target_ref[:, cols]).astype(BF16)


def collect_sum(index_ref, table, hot, even, odd, total, size):
    chunks = 4096 // size

    def collect(base, picked):
        for u in range(size):
            picked[u : u + 1, :] = table[pl.ds(index_ref[0, base + u], 1), :]

    def add(base, picked):
        high, low = split(picked[...])
        both = jnp.concatenate([high, low], axis=1)
        cols = pl.ds(pl.multiple_of(base, size), size)
        total[...] += jnp.dot(hot[:, cols], both, preferred_element_type=F32)

    total[...] = jnp.zeros_like(total)
    collect(0, even)

    def body(step, carry):
        base = step * (2 * size)
        collect(base + size, odd)
        add(base, even)
        collect(base + 2 * size, even)
        add(base + size, odd)
        return carry

    lax.fori_loop(0, chunks // 2 - 1, body, 0)
    collect(4096 - size, odd)
    add(4096 - 2 * size, even)
    add(4096 - size, odd)


def far_out(total, out_ref):
    for j in range(4):
        rows = slice(128 * j, 128 * j + 128)
        out_ref[:, rows] = (total[rows, :128] + total[rows, 128:]).T[0:121]


MESH = pl.DeviceIdType.MESH
GROUPS = 64


def each_other(g, skip, act):
    columns = [lax.rem(g // 16 + d, 4) * 16 for d in range(4)]
    rows = [lax.rem((g // 2) % 8 + d, 8) * 2 for d in range(8)]
    cores = [g % 2, 1 - g % 2]
    for dy in (4, 3, 5, 2, 6, 1, 7, 0):
        for dx in (2, 1, 3, 0):
            for dc in (0, 1):
                if (dx, dy, dc) != (0, 0, 0):
                    other = columns[dx] + rows[dy] + cores[dc]
                    if skip is None:
                        act(other)
                    else:
                        pl.when(other != skip)(functools.partial(act, other))


def kernel(
    coords_hbm,
    charges_hbm,
    mult_hbm,
    ops_hbm,
    send_hbm,
    near_hbm,
    source_hbm,
    target_hbm,
    kind_hbm,
    far_rows,
    pot_rows,
    coords,
    charges,
    mult,
    ops,
    sends,
    near,
    entry_source,
    entry_target,
    entry_kind,
    index_row,
    index,
    stage,
    window,
    tile,
    spot,
    hots,
    cells,
    sources,
    pot,
    flip,
    held,
    outgoing,
    received,
    pad,
    first,
    second,
    table,
    hot,
    even,
    odd,
    total,
    load_sem,
    halo_send,
    halo_recv,
    rows_send,
    rows_recv,
):
    slabs = lax.axis_size("slab")
    s, g = lax.axis_index("slab"), lax.axis_index("grp")
    barrier = pltpu.get_barrier_semaphore()

    def greet(other):
        pl.semaphore_signal(barrier, inc=1, device_id={"grp": other}, device_id_type=MESH)

    loads = [
        pltpu.make_async_copy(source, target, load_sem.at[i])
        for i, (source, target) in enumerate(
            [
                (mult_hbm, mult),
                (send_hbm, sends),
                (coords_hbm, coords),
                (charges_hbm, charges),
                (near_hbm, near),
                (ops_hbm, ops),
                (source_hbm, entry_source),
                (kind_hbm, entry_kind),
                (target_hbm, entry_target),
            ]
        )
    ]
    for load in loads:
        load.start()

    @pl.when(s > 0)
    def _():
        pl.semaphore_signal(barrier, inc=1, device_id={"slab": s - 1}, device_id_type=MESH)

    @pl.when(s < slabs - 1)
    def _():
        pl.semaphore_signal(barrier, inc=1, device_id={"slab": s + 1}, device_id_type=MESH)

    late = (s == 0) & (g == 0)
    meets_late = (s == 0) & (g != 0)

    def each(act):
        @pl.when(s == 0)
        def _():
            each_other(g, 0, act)

        @pl.when(s != 0)
        def _():
            each_other(g, None, act)

    pl.when(jnp.logical_not(late))(functools.partial(each, greet))

    loads[0].wait()
    loads[1].wait()
    send_rows(mult, sends, held, outgoing)
    loads[2].wait()
    loads[3].wait()
    own = window.at[4:8]
    own_window(coords, charges, stage, own)

    inner = jnp.where(s > 0, 1, 0) + jnp.where(s < slabs - 1, 1, 0)
    pl.semaphore_wait(barrier, GROUPS - 1 - jnp.where(meets_late, 1, 0) + inner)

    @pl.when(meets_late)
    def _():
        greet(0)

    up = pltpu.make_async_remote_copy(
        src_ref=own,
        dst_ref=window.at[0:4],
        send_sem=halo_send.at[0],
        recv_sem=halo_recv.at[0],
        device_id={"slab": jnp.minimum(s + 1, slabs - 1)},
        device_id_type=MESH,
    )
    down = pltpu.make_async_remote_copy(
        src_ref=own,
        dst_ref=window.at[8:12],
        send_sem=halo_send.at[1],
        recv_sem=halo_recv.at[1],
        device_id={"slab": jnp.maximum(s - 1, 0)},
        device_id_type=MESH,
    )

    @pl.when(s < slabs - 1)
    def _():
        up.start()

    @pl.when(s > 0)
    def _():
        down.start()

    y = (g // 2) % 8
    mine = pl.ds(pl.multiple_of(y * 128 + (g // 16) * 32 + (g % 2) * 16, 16), 16)

    def rows_copy(other):
        return pltpu.make_async_remote_copy(
            src_ref=outgoing.at[pl.ds(pl.multiple_of(16 * other, 16), 16)],
            dst_ref=received.at[mine],
            send_sem=rows_send,
            recv_sem=rows_recv.at[y // 2],
            device_id={"grp": other},
            device_id_type=MESH,
        )

    each(lambda other: rows_copy(other).start())

    @pl.when(late)
    def _():
        each_other(g, None, greet)

    received[mine, :] = outgoing[pl.ds(pl.multiple_of(16 * g, 16), 16), :]

    loads[4].wait()
    near_index(near, tile, spot)
    near_hot(spot, hots)
    loads[5].wait()
    operator_parts(ops, pad, first, second)
    loads[6].wait()
    loads[7].wait()
    source = entry_source[...]
    place = ((source >> 5) & 7) * 128 + (source >> 8) * 32 + (source & 31)
    index_row[...] = entry_kind[...] * 1024 + place
    index_load = pltpu.make_async_copy(index_row, index, load_sem.at[9])
    index_load.start()
    loads[8].wait()
    target_table(entry_target, hot)
    near_table(window, cells, 1)

    @pl.when(s == 0)
    def _():
        window[0:4] = jnp.zeros((4, 64, 128), F32)

    @pl.when(s == slabs - 1)
    def _():
        window[8:12] = jnp.zeros((4, 64, 128), F32)

    @pl.when(s > 0)
    def _():
        up.wait_recv()

    @pl.when(s < slabs - 1)
    def _():
        down.wait_recv()

    near_table(window, cells, 0)
    near_table(window, cells, 2)
    near_gather(cells, tile, hots, sources)

    near_sum(own, sources, pot)
    near_out(pot, flip, pot_rows)
    index_load.wait()

    def arrived(count, k):
        block = pl.ds(0, 16 * count)
        return pltpu.make_async_remote_copy(
            src_ref=outgoing.at[block],
            dst_ref=received.at[block],
            send_sem=rows_send,
            recv_sem=rows_recv.at[k],
            device_id={"grp": lax.rem(g + 1, GROUPS)},
            device_id_type=MESH,
        )

    for i, turn in enumerate((2, 1, 3, 0)):
        k = lax.rem(jnp.where(s == 0, 1 + i, y // 2 + turn), 4)
        if i == 3:

            @pl.when(meets_late)
            def _():
                pl.semaphore_wait(barrier, 1)
                rows_copy(0).start()

        @pl.when(y // 2 == k)
        def _():
            arrived(15, k).wait_recv()

        @pl.when(y // 2 != k)
        def _():
            arrived(16, k).wait_recv()

        start = pl.multiple_of(256 * k, 256)
        translate(received[pl.ds(start, 256), :], first, second, table, start)

    collect_sum(index, table, hot, even, odd, total, 512)
    far_out(total, far_rows)

    arrived(GROUPS - 1, 0).wait_send()

    @pl.when(s < slabs - 1)
    def _():
        up.wait_send()

    @pl.when(s > 0)
    def _():
        down.wait_send()


def shards(
    coords,
    charges,
    multipoles,
    operators,
    send_list,
    near_list,
    m2l_source,
    m2l_target,
    m2l_operator,
):
    operands = (
        coords,
        charges.reshape(64, 128),
        multipoles,
        jnp.transpose(operators, (1, 0, 2)),
        send_list,
        near_list.T,
        m2l_source,
        m2l_target,
        m2l_operator,
    )
    hbm = pl.BlockSpec(memory_space=pltpu.HBM)
    vmem, dma = pltpu.VMEM, pltpu.SemaphoreType.DMA
    far, pot = pl.pallas_call(
        kernel,
        out_shape=[vmem((121, 512), F32), vmem((64, 128), F32)],
        in_specs=[hbm] * 9,
        out_specs=[pl.BlockSpec(memory_space=vmem)] * 2,
        scratch_shapes=[
            vmem((3, 8192), F32),
            vmem((64, 128), F32),
            vmem((121, 512), F32),
            vmem((121, 8, 121), F32),
            vmem((1, 1024), I32),
            vmem((8, 512), I32),
            vmem((1, 4096), I32),
            vmem((1, 4096), I32),
            vmem((1, 4096), I32),
            vmem((1, 4096), I32),
            pltpu.SMEM((1, 4096), I32),
            vmem((2, 128, 128), F32),
            vmem((12, 64, 128), F32),
            vmem((4, 8, 128), I32),
            vmem((4, 8, 128), I32),
            vmem((16, 256, 256), BF16),
            vmem((768, 256), BF16),
            vmem((4, 8, 64, 128), F32),
            vmem((4, 16, 128), F32),
            vmem((128, 128), F32),
            vmem((128, 512), F32),
            vmem((1024, 128), F32),
            vmem((1024, 128), F32),
            vmem((128, 128), F32),
            vmem((4, 256, 256), BF16),
            vmem((4, 256, 128), BF16),
            vmem((8192, 128), F32),
            vmem((512, 4096), BF16),
            vmem((512, 128), F32),
            vmem((512, 128), F32),
            vmem((512, 256), F32),
            dma((10,)),
            dma((2,)),
            dma((2,)),
            dma,
            dma((4,)),
        ],
        compiler_params=pltpu.CompilerParams(
            collective_id=0, has_side_effects=True, vmem_limit_bytes=48 * 2**20
        ),
    )(*(pltpu.with_memory_space_constraint(x, pltpu.HBM) for x in operands))
    return far, pot.reshape(-1)


def solution(mesh):
    both = ("slab", "grp")
    return jax.shard_map(
        shards,
        mesh=mesh,
        in_specs=(P(None, both), P(both), P(None, both), P()) + (P(both, None),) * 5,
        out_specs=(P(None, both), P(both)),
        check_vma=False,
    )
```

```python
import functools
import jax
import jax.numpy as jnp
from jax import lax
from jax.experimental import pallas as pl
from jax.experimental.pallas import tpu as pltpu
from jax.sharding import PartitionSpec as P

SOFT2 = 0.0625
F32, BF16, I32 = jnp.float32, jnp.bfloat16, jnp.int32


def split(x):
    high = x.astype(BF16)
    return high, (x - high.astype(F32)).astype(BF16)


def send_rows(mult_ref, send_ref, held, out_ref):
    held[...] = jnp.zeros_like(held)
    held[0:121, :] = mult_ref[...]
    high, low = split(held[...])
    both = jnp.concatenate([high, low], axis=0)
    for k in range(4):
        cols = slice(256 * k, 256 * k + 256)
        pick = (lax.broadcasted_iota(I32, (512, 256), 0) == send_ref[:, cols]).astype(BF16)
        got = jnp.dot(both, pick, preferred_element_type=F32)
        out_ref[cols, :] = (got[:128] + got[128:]).T


def own_window(coords_ref, charges_ref, stage, own):
    for c in range(64):
        for q in range(3):
            stage[q // 2, pl.ds(64 * (q % 2) + c, 1), :] = coords_ref[q : q + 1, 128 * c : 128 * c + 128]
    stage[1, 64:128, :] = charges_ref[...]
    lane = lax.broadcasted_iota(I32, (16, 128), 1)
    for h in range(2):
        t = stage[h].T
        for j in range(4):
            left, right = t[32 * j : 32 * j + 16], t[32 * j + 16 : 32 * j + 32]
            own[j, 32 * h : 32 * h + 16, :] = jnp.where(lane < 64, left, pltpu.roll(right, 64, 1))
            own[j, 32 * h + 16 : 32 * h + 32, :] = jnp.where(lane < 64, pltpu.roll(left, 64, 1), right)


def take(x, index):
    return jnp.take_along_axis(x, index, axis=1)


def near_index(near_ref, tile_ref, lane_ref):
    lane = lax.broadcasted_iota(I32, (8, 128), 1)
    c, half = lane & 63, lane >> 6
    for j in range(4):
        spot = 8 * (c & 15) + 2 * j + half
        w = jnp.zeros((8, 128), I32)
        for k in range(4):
            w = jnp.where((c >> 4) == k, take(near_ref[:, 128 * k : 128 * k + 128], spot), w)
        leaf = w & 511
        tile_ref[j] = (w >> 9) * 4 + ((leaf & 7) >> 1)
        lane_ref[j] = (leaf & 1) * 64 + (leaf >> 3)


def near_hot(lane_ref, hots):
    spots = lax.broadcasted_iota(I32, (128, 128), 0)
    for step in range(16):
        j, n = step // 4, 2 * (step % 4)
        for u in range(2):
            hit = (spots == lane_ref[j, n + u : n + u + 1, :]).astype(BF16)
            hots[step, 0:128, 128 * u : 128 * u + 128] = hit
            hots[step, 128:256, 128 * u : 128 * u + 128] = hit


def near_table(window, cells, block):
    rows = slice(256 * block, 256 * block + 256)
    high, low = split(window[4 * block : 4 * block + 4].reshape(256, 128))
    cells[rows, 0:128] = high
    cells[rows, 128:256] = low


def near_gather(cells, tile_ref, hots, sources):
    def body(step, carry):
        j, n = step // 4, 2 * (step % 4)
        got = jnp.dot(cells[...], hots[step], preferred_element_type=F32)
        for u in range(2):
            tile = jnp.broadcast_to(tile_ref[j, pl.ds(n + u, 1), :], (8, 128))
            masks = [tile == k for k in range(1, 12)]
            cols = slice(128 * u, 128 * u + 128)
            for row in range(0, 64, 8):
                value = got[row : row + 8, cols]
                for k in range(1, 12):
                    value = jnp.where(masks[k - 1], got[64 * k + row : 64 * k + row + 8, cols], value)
                sources[j, n + u, row : row + 8, :] = value
        return carry

    lax.fori_loop(0, 16, body, 0)


def near_sum(own, sources, pot):
    def body(step, carry):
        j, i = step // 8, step % 8
        targets = [
            [jnp.broadcast_to(own[j, pl.ds(16 * q + i + 8 * u, 1), :], (8, 128)) for q in range(3)]
            for u in range(2)
        ]
        total = [jnp.zeros((8, 128), F32) for _ in range(2)]
        for n in range(8):
            for h in range(2):
                s = [sources[j, n, 16 * q + 8 * h : 16 * q + 8 * h + 8, :] for q in range(4)]
                for u in range(2):
                    dx, dy, dz = (targets[u][q] - s[q] for q in range(3))
                    total[u] = total[u] + s[3] * lax.rsqrt(dx * dx + dy * dy + dz * dz + SOFT2)
        for u in range(2):
            pot[j, pl.ds(i + 8 * u, 1), :] = jnp.sum(total[u], axis=0, keepdims=True)
        return carry

    lax.fori_loop(0, 32, body, 0)


def near_out(pot, flip, out_ref):
    for j in range(4):
        flip[32 * j : 32 * j + 16, :] = pot[j]
        flip[32 * j + 16 : 32 * j + 32, :] = pltpu.roll(pot[j], 64, 1)
    out_ref[...] = flip[...].T[0:64]


def operator_parts(ops_ref, pad, first, second):
    pad[...] = jnp.zeros_like(pad)
    for o in range(8):
        pad[0:121, 0:121] = ops_ref[:, o, :]
        high, low = split(pad[...])
        rows = slice(128 * (o % 2), 128 * (o % 2) + 128)
        first[o // 2, rows, 0:128] = high
        first[o // 2, rows, 128:256] = high
        second[o // 2, rows, :] = low


NT = (((1,), (1,)), ((), ()))


def translate(rows, first, second, table, start):
    count = rows.shape[0]
    high, low = split(rows)
    both = jnp.concatenate([high, low], axis=1)
    for k in range(4):
        got = lax.dot_general(both, first[k], NT, preferred_element_type=F32)
        got = got + lax.dot_general(high, second[k], NT, preferred_element_type=F32)
        table[pl.ds(2 * k * 1024 + start, count), :] = got[:, :128]
        table[pl.ds((2 * k + 1) * 1024 + start, count), :] = got[:, 128:]


def target_table(target_ref, hot):
    for k in range(16):
        cols = slice(256 * k, 256 * k + 256)
        hot[:, cols] = (lax.broadcasted_iota(I32, (512, 256), 0) == target_ref[:, cols]).astype(BF16)


def collect_sum(index_ref, table, hot, even, odd, total, size):
    chunks = 4096 // size

    def collect(base, picked):
        for u in range(size):
            picked[u : u + 1, :] = table[pl.ds(index_ref[0, base + u], 1), :]

    def add(base, picked):
        high, low = split(picked[...])
        both = jnp.concatenate([high, low], axis=1)
        cols = pl.ds(pl.multiple_of(base, size), size)
        total[...] += jnp.dot(hot[:, cols], both, preferred_element_type=F32)

    total[...] = jnp.zeros_like(total)
    collect(0, even)

    def body(step, carry):
        base = step * (2 * size)
        collect(base + size, odd)
        add(base, even)
        collect(base + 2 * size, even)
        add(base + size, odd)
        return carry

    lax.fori_loop(0, chunks // 2 - 1, body, 0)
    collect(4096 - size, odd)
    add(4096 - 2 * size, even)
    add(4096 - size, odd)


def far_out(total, out_ref):
    for j in range(4):
        rows = slice(128 * j, 128 * j + 128)
        out_ref[:, rows] = (total[rows, :128] + total[rows, 128:]).T[0:121]


MESH = pl.DeviceIdType.MESH
GROUPS = 64


def each_other(g, skip, act, early=None):
    columns = [lax.rem(g // 16 + d, 4) * 16 for d in range(4)]
    rows = [lax.rem((g // 2) % 8 + d, 8) * 2 for d in range(8)]
    cores = [g % 2, 1 - g % 2]
    for dy in (4, 3, 5, 2, 6, 1, 7, 0):

        def row(dy=dy):
            for dx in (2, 1, 3, 0):
                for dc in (0, 1):
                    if (dx, dy, dc) != (0, 0, 0):
                        other = columns[dx] + rows[dy] + cores[dc]
                        if skip is None:
                            act(other)
                        else:
                            pl.when(other != skip)(functools.partial(act, other))

        if early is None:
            row()
        else:
            pl.when(rows[dy] < 8 if early else rows[dy] >= 8)(row)


def kernel(
    coords_hbm,
    charges_hbm,
    mult_hbm,
    ops_hbm,
    send_hbm,
    near_hbm,
    source_hbm,
    target_hbm,
    kind_hbm,
    far_rows,
    pot_rows,
    coords,
    charges,
    mult,
    ops,
    sends,
    near,
    entry_source,
    entry_target,
    entry_kind,
    index_row,
    index,
    stage,
    window,
    tile,
    spot,
    hots,
    cells,
    sources,
    pot,
    flip,
    held,
    outgoing,
    received,
    pad,
    first,
    second,
    table,
    hot,
    even,
    odd,
    total,
    load_sem,
    halo_send,
    halo_recv,
    rows_send,
    rows_recv,
):
    slabs = lax.axis_size("slab")
    s, g = lax.axis_index("slab"), lax.axis_index("grp")
    barrier = pltpu.get_barrier_semaphore()

    def greet(other):
        pl.semaphore_signal(barrier, inc=1, device_id={"grp": other}, device_id_type=MESH)

    loads = [
        pltpu.make_async_copy(source, target, load_sem.at[i])
        for i, (source, target) in enumerate(
            [
                (mult_hbm, mult),
                (send_hbm, sends),
                (coords_hbm, coords),
                (charges_hbm, charges),
                (near_hbm, near),
                (ops_hbm, ops),
                (source_hbm, entry_source),
                (kind_hbm, entry_kind),
                (target_hbm, entry_target),
            ]
        )
    ]
    for load in loads:
        load.start()

    @pl.when(s > 0)
    def _():
        pl.semaphore_signal(barrier, inc=1, device_id={"slab": s - 1}, device_id_type=MESH)

    @pl.when(s < slabs - 1)
    def _():
        pl.semaphore_signal(barrier, inc=1, device_id={"slab": s + 1}, device_id_type=MESH)

    late = (s == 0) & (g == 0)
    meets_late = (s == 0) & (g != 0)

    def each(act, early=None):
        @pl.when(s == 0)
        def _():
            each_other(g, 0, act, early)

        @pl.when(s != 0)
        def _():
            each_other(g, None, act, early)

    pl.when(jnp.logical_not(late))(functools.partial(each, greet))

    loads[0].wait()
    loads[1].wait()
    send_rows(mult, sends, held, outgoing)
    loads[2].wait()
    loads[3].wait()
    own = window.at[4:8]
    own_window(coords, charges, stage, own)

    inner = jnp.where(s > 0, 1, 0) + jnp.where(s < slabs - 1, 1, 0)
    pl.semaphore_wait(barrier, GROUPS - 1 - jnp.where(meets_late, 1, 0) + inner)

    @pl.when(meets_late)
    def _():
        greet(0)

    up = pltpu.make_async_remote_copy(
        src_ref=own,
        dst_ref=window.at[0:4],
        send_sem=halo_send.at[0],
        recv_sem=halo_recv.at[0],
        device_id={"slab": jnp.minimum(s + 1, slabs - 1)},
        device_id_type=MESH,
    )
    down = pltpu.make_async_remote_copy(
        src_ref=own,
        dst_ref=window.at[8:12],
        send_sem=halo_send.at[1],
        recv_sem=halo_recv.at[1],
        device_id={"slab": jnp.maximum(s - 1, 0)},
        device_id_type=MESH,
    )

    @pl.when(s < slabs - 1)
    def _():
        up.start()

    @pl.when(s > 0)
    def _():
        down.start()

    y = (g // 2) % 8
    mine = pl.ds(pl.multiple_of(y * 128 + (g // 16) * 32 + (g % 2) * 16, 16), 16)

    def rows_copy(other):
        return pltpu.make_async_remote_copy(
            src_ref=outgoing.at[pl.ds(pl.multiple_of(16 * other, 16), 16)],
            dst_ref=received.at[mine],
            send_sem=rows_send,
            recv_sem=rows_recv.at[jnp.where(late, 4, y // 2)],
            device_id={"grp": other},
            device_id_type=MESH,
        )

    each(lambda other: rows_copy(other).start(), True)
    each(lambda other: rows_copy(other).start(), False)

    received[mine, :] = outgoing[pl.ds(pl.multiple_of(16 * g, 16), 16), :]

    loads[4].wait()
    near_index(near, tile, spot)
    near_hot(spot, hots)
    loads[5].wait()
    operator_parts(ops, pad, first, second)
    loads[6].wait()
    loads[7].wait()
    source = entry_source[...]
    place = ((source >> 5) & 7) * 128 + (source >> 8) * 32 + (source & 31)
    index_row[...] = entry_kind[...] * 1024 + place
    index_load = pltpu.make_async_copy(index_row, index, load_sem.at[9])
    index_load.start()
    loads[8].wait()
    target_table(entry_target, hot)
    near_table(window, cells, 1)

    @pl.when(s == 0)
    def _():
        window[0:4] = jnp.zeros((4, 64, 128), F32)

    @pl.when(s == slabs - 1)
    def _():
        window[8:12] = jnp.zeros((4, 64, 128), F32)

    @pl.when(s > 0)
    def _():
        up.wait_recv()

    @pl.when(s < slabs - 1)
    def _():
        down.wait_recv()

    near_table(window, cells, 0)
    near_table(window, cells, 2)
    near_gather(cells, tile, hots, sources)

    near_sum(own, sources, pot)
    near_out(pot, flip, pot_rows)
    index_load.wait()

    def arrived(count, k):
        block = pl.ds(0, 16 * count)
        return pltpu.make_async_remote_copy(
            src_ref=outgoing.at[block],
            dst_ref=received.at[block],
            send_sem=rows_send,
            recv_sem=rows_recv.at[k],
            device_id={"grp": lax.rem(g + 1, GROUPS)},
            device_id_type=MESH,
        )

    for i, turn in enumerate((2, 1, 3, 0)):
        k = lax.rem(jnp.where(s == 0, 1 + i, y // 2 + turn), 4)
        if i == 3:

            @pl.when(meets_late)
            def _():
                arrived(1, 4).wait_recv()
                rows_copy(0).start()

        missing = jnp.where(y // 2 == k, 1, 0)
        if i == 3:
            missing = missing + jnp.where(meets_late, 1, 0)
        for count in (14, 15, 16):

            @pl.when(missing == 16 - count)
            def _():
                arrived(count, k).wait_recv()

        start = pl.multiple_of(256 * k, 256)
        translate(received[pl.ds(start, 256), :], first, second, table, start)

    collect_sum(index, table, hot, even, odd, total, 512)
    far_out(total, far_rows)

    arrived(GROUPS - 1, 0).wait_send()

    @pl.when(s < slabs - 1)
    def _():
        up.wait_send()

    @pl.when(s > 0)
    def _():
        down.wait_send()


def shards(
    coords,
    charges,
    multipoles,
    operators,
    send_list,
    near_list,
    m2l_source,
    m2l_target,
    m2l_operator,
):
    operands = (
        coords,
        charges.reshape(64, 128),
        multipoles,
        jnp.transpose(operators, (1, 0, 2)),
        send_list,
        near_list.T,
        m2l_source,
        m2l_target,
        m2l_operator,
    )
    hbm = pl.BlockSpec(memory_space=pltpu.HBM)
    vmem, dma = pltpu.VMEM, pltpu.SemaphoreType.DMA
    far, pot = pl.pallas_call(
        kernel,
        out_shape=[vmem((121, 512), F32), vmem((64, 128), F32)],
        in_specs=[hbm] * 9,
        out_specs=[pl.BlockSpec(memory_space=vmem)] * 2,
        scratch_shapes=[
            vmem((3, 8192), F32),
            vmem((64, 128), F32),
            vmem((121, 512), F32),
            vmem((121, 8, 121), F32),
            vmem((1, 1024), I32),
            vmem((8, 512), I32),
            vmem((1, 4096), I32),
            vmem((1, 4096), I32),
            vmem((1, 4096), I32),
            vmem((1, 4096), I32),
            pltpu.SMEM((1, 4096), I32),
            vmem((2, 128, 128), F32),
            vmem((12, 64, 128), F32),
            vmem((4, 8, 128), I32),
            vmem((4, 8, 128), I32),
            vmem((16, 256, 256), BF16),
            vmem((768, 256), BF16),
            vmem((4, 8, 64, 128), F32),
            vmem((4, 16, 128), F32),
            vmem((128, 128), F32),
            vmem((128, 512), F32),
            vmem((1024, 128), F32),
            vmem((1024, 128), F32),
            vmem((128, 128), F32),
            vmem((4, 256, 256), BF16),
            vmem((4, 256, 128), BF16),
            vmem((8192, 128), F32),
            vmem((512, 4096), BF16),
            vmem((512, 128), F32),
            vmem((512, 128), F32),
            vmem((512, 256), F32),
            dma((10,)),
            dma((2,)),
            dma((2,)),
            dma,
            dma((5,)),
        ],
        compiler_params=pltpu.CompilerParams(
            collective_id=0, has_side_effects=True, vmem_limit_bytes=48 * 2**20
        ),
    )(*(pltpu.with_memory_space_constraint(x, pltpu.HBM) for x in operands))
    return far, pot.reshape(-1)


def solution(mesh):
    both = ("slab", "grp")
    return jax.shard_map(
        shards,
        mesh=mesh,
        in_specs=(P(None, both), P(both), P(None, both), P()) + (P(both, None),) * 5,
        out_specs=(P(None, both), P(both)),
        check_vma=False,
    )
```

```python
import functools
import jax
import jax.numpy as jnp
from jax import lax
from jax.experimental import pallas as pl
from jax.experimental.pallas import tpu as pltpu
from jax.sharding import PartitionSpec as P

SOFT2 = 0.0625
F32, BF16, I32 = jnp.float32, jnp.bfloat16, jnp.int32


def split(x):
    high = x.astype(BF16)
    return high, (x - high.astype(F32)).astype(BF16)


def send_rows(mult_ref, send_ref, held, out_ref):
    held[...] = jnp.zeros_like(held)
    held[0:121, :] = mult_ref[...]
    high, low = split(held[...])
    both = jnp.concatenate([high, low], axis=0)
    for k in range(4):
        cols = slice(256 * k, 256 * k + 256)
        pick = (lax.broadcasted_iota(I32, (512, 256), 0) == send_ref[:, cols]).astype(BF16)
        got = jnp.dot(both, pick, preferred_element_type=F32)
        out_ref[cols, :] = (got[:128] + got[128:]).T


def own_window(coords_ref, charges_ref, stage, own):
    for c in range(64):
        for q in range(3):
            stage[q // 2, pl.ds(64 * (q % 2) + c, 1), :] = coords_ref[q : q + 1, 128 * c : 128 * c + 128]
    stage[1, 64:128, :] = charges_ref[...]
    lane = lax.broadcasted_iota(I32, (16, 128), 1)
    for h in range(2):
        t = stage[h].T
        for j in range(4):
            left, right = t[32 * j : 32 * j + 16], t[32 * j + 16 : 32 * j + 32]
            own[j, 32 * h : 32 * h + 16, :] = jnp.where(lane < 64, left, pltpu.roll(right, 64, 1))
            own[j, 32 * h + 16 : 32 * h + 32, :] = jnp.where(lane < 64, pltpu.roll(left, 64, 1), right)


def take(x, index):
    return jnp.take_along_axis(x, index, axis=1)


def near_index(near_ref, tile_ref, lane_ref):
    lane = lax.broadcasted_iota(I32, (8, 128), 1)
    c, half = lane & 63, lane >> 6
    for j in range(4):
        spot = 8 * (c & 15) + 2 * j + half
        w = jnp.zeros((8, 128), I32)
        for k in range(4):
            w = jnp.where((c >> 4) == k, take(near_ref[:, 128 * k : 128 * k + 128], spot), w)
        leaf = w & 511
        tile_ref[j] = (w >> 9) * 4 + ((leaf & 7) >> 1)
        lane_ref[j] = (leaf & 1) * 64 + (leaf >> 3)


def near_hot(lane_ref, hots):
    spots = lax.broadcasted_iota(I32, (128, 128), 0)
    for step in range(16):
        j, n = step // 4, 2 * (step % 4)
        for u in range(2):
            hit = (spots == lane_ref[j, n + u : n + u + 1, :]).astype(BF16)
            hots[step, 0:128, 128 * u : 128 * u + 128] = hit
            hots[step, 128:256, 128 * u : 128 * u + 128] = hit


def near_table(window, cells, block):
    rows = slice(256 * block, 256 * block + 256)
    high, low = split(window[4 * block : 4 * block + 4].reshape(256, 128))
    cells[rows, 0:128] = high
    cells[rows, 128:256] = low


def near_gather(cells, tile_ref, hots, sources):
    def body(step, carry):
        j, n = step // 4, 2 * (step % 4)
        got = jnp.dot(cells[...], hots[step], preferred_element_type=F32)
        for u in range(2):
            tile = jnp.broadcast_to(tile_ref[j, pl.ds(n + u, 1), :], (8, 128))
            masks = [tile == k for k in range(1, 12)]
            cols = slice(128 * u, 128 * u + 128)
            for row in range(0, 64, 8):
                value = got[row : row + 8, cols]
                for k in range(1, 12):
                    value = jnp.where(masks[k - 1], got[64 * k + row : 64 * k + row + 8, cols], value)
                sources[j, n + u, row : row + 8, :] = value
        return carry

    lax.fori_loop(0, 16, body, 0)


def near_sum(own, sources, pot):
    def body(step, carry):
        j, i = step // 8, step % 8
        targets = [
            [jnp.broadcast_to(own[j, pl.ds(16 * q + i + 8 * u, 1), :], (8, 128)) for q in range(3)]
            for u in range(2)
        ]
        total = [jnp.zeros((8, 128), F32) for _ in range(2)]
        for n in range(8):
            for h in range(2):
                s = [sources[j, n, 16 * q + 8 * h : 16 * q + 8 * h + 8, :] for q in range(4)]
                for u in range(2):
                    dx, dy, dz = (targets[u][q] - s[q] for q in range(3))
                    total[u] = total[u] + s[3] * lax.rsqrt(dx * dx + dy * dy + dz * dz + SOFT2)
        for u in range(2):
            pot[j, pl.ds(i + 8 * u, 1), :] = jnp.sum(total[u], axis=0, keepdims=True)
        return carry

    lax.fori_loop(0, 32, body, 0)


def near_out(pot, flip, out_ref):
    for j in range(4):
        flip[32 * j : 32 * j + 16, :] = pot[j]
        flip[32 * j + 16 : 32 * j + 32, :] = pltpu.roll(pot[j], 64, 1)
    out_ref[...] = flip[...].T[0:64]


def operator_parts(ops_ref, pad, first, second):
    pad[...] = jnp.zeros_like(pad)
    for o in range(8):
        pad[0:121, 0:121] = ops_ref[:, o, :]
        high, low = split(pad[...])
        rows = slice(128 * (o % 2), 128 * (o % 2) + 128)
        first[o // 2, rows, 0:128] = high
        first[o // 2, rows, 128:256] = high
        second[o // 2, rows, :] = low


NT = (((1,), (1,)), ((), ()))


def translate(rows, first, second, table, start):
    count = rows.shape[0]
    high, low = split(rows)
    both = jnp.concatenate([high, low], axis=1)
    for k in range(4):
        got = lax.dot_general(both, first[k], NT, preferred_element_type=F32)
        got = got + lax.dot_general(high, second[k], NT, preferred_element_type=F32)
        table[pl.ds(2 * k * 1024 + start, count), :] = got[:, :128]
        table[pl.ds((2 * k + 1) * 1024 + start, count), :] = got[:, 128:]


def target_table(target_ref, hot):
    for k in range(16):
        cols = slice(256 * k, 256 * k + 256)
        hot[:, cols] = (lax.broadcasted_iota(I32, (512, 256), 0) == target_ref[:, cols]).astype(BF16)


def collect_sum(index_ref, table, hot, even, odd, total, size):
    chunks = 4096 // size

    def collect(base, picked):
        for u in range(size):
            picked[u : u + 1, :] = table[pl.ds(index_ref[0, base + u], 1), :]

    def add(base, picked):
        high, low = split(picked[...])
        both = jnp.concatenate([high, low], axis=1)
        total[...] += jnp.dot(hot[:, base : base + size], both, preferred_element_type=F32)

    total[...] = jnp.zeros_like(total)
    collect(0, even)

    for k in range(1, chunks + 1):
        if k < chunks:
            collect(k * size, odd if k % 2 else even)
        add((k - 1) * size, even if k % 2 else odd)


def far_out(total, out_ref):
    for j in range(4):
        rows = slice(128 * j, 128 * j + 128)
        out_ref[:, rows] = (total[rows, :128] + total[rows, 128:]).T[0:121]


MESH = pl.DeviceIdType.MESH
GROUPS = 64
SECOND = 5


def each_other(g, skip, act, early=None):
    columns = [lax.rem(g // 16 + d, 4) * 16 for d in range(4)]
    rows = [lax.rem((g // 2) % 8 + d, 8) * 2 for d in range(8)]
    cores = [g % 2, 1 - g % 2]
    for dy in (4, 3, 5, 2, 6, 1, 7, 0):

        def row(dy=dy):
            for dx in (2, 1, 3, 0):
                for dc in (0, 1):
                    if (dx, dy, dc) != (0, 0, 0):
                        other = columns[dx] + rows[dy] + cores[dc]
                        if skip is None:
                            act(other)
                        else:
                            pl.when(other != skip)(functools.partial(act, other))

        if early is None:
            row()
        else:
            pl.when(rows[dy] < 8 if early else rows[dy] >= 8)(row)


def kernel(
    coords_hbm,
    charges_hbm,
    mult_hbm,
    ops_hbm,
    send_hbm,
    near_hbm,
    source_hbm,
    target_hbm,
    kind_hbm,
    far_rows,
    pot_rows,
    coords,
    charges,
    mult,
    ops,
    sends,
    near,
    entry_source,
    entry_target,
    entry_kind,
    index_row,
    index,
    stage,
    window,
    tile,
    spot,
    hots,
    cells,
    sources,
    pot,
    flip,
    held,
    outgoing,
    received,
    pad,
    first,
    second,
    table,
    hot,
    even,
    odd,
    total,
    load_sem,
    halo_send,
    halo_recv,
    rows_send,
    rows_recv,
):
    slabs = lax.axis_size("slab")
    s, g = lax.axis_index("slab"), lax.axis_index("grp")
    barrier = pltpu.get_barrier_semaphore()

    def greet(other):
        pl.semaphore_signal(barrier, inc=1, device_id={"grp": other}, device_id_type=MESH)

    loads = [
        pltpu.make_async_copy(source, target, load_sem.at[i])
        for i, (source, target) in enumerate(
            [
                (mult_hbm, mult),
                (send_hbm, sends),
                (coords_hbm, coords),
                (charges_hbm, charges),
                (near_hbm, near),
                (ops_hbm, ops),
                (source_hbm, entry_source),
                (kind_hbm, entry_kind),
                (target_hbm, entry_target),
            ]
        )
    ]
    for load in loads:
        load.start()

    def greet_slab(other):
        pl.semaphore_signal(barrier, inc=1, device_id={"slab": other}, device_id_type=MESH)

    upper = s < slabs - 1
    upper_second = upper & (s < SECOND) & ((s > 0) | (g > 0))
    is_second = (s > 0) & (s <= SECOND) & ((s > 1) | (g > 0))

    @pl.when((s > 0) & jnp.logical_not(is_second))
    def _():
        greet_slab(s - 1)

    @pl.when(upper & jnp.logical_not(upper_second))
    def _():
        greet_slab(s + 1)

    late = (s == 0) & (g == 0)
    meets_late = (s == 0) & (g != 0)

    def each(act, early=None):
        @pl.when(s == 0)
        def _():
            each_other(g, 0, act, early)

        @pl.when(s != 0)
        def _():
            each_other(g, None, act, early)

    pl.when(jnp.logical_not(late))(functools.partial(each, greet))

    loads[0].wait()
    loads[1].wait()
    send_rows(mult, sends, held, outgoing)
    loads[2].wait()
    loads[3].wait()
    own = window.at[4:8]
    own_window(coords, charges, stage, own)

    inner = jnp.where(s > 0, 1, 0) + jnp.where(upper & jnp.logical_not(upper_second), 1, 0)
    pl.semaphore_wait(barrier, GROUPS - 1 - jnp.where(meets_late, 1, 0) + inner)

    @pl.when(upper_second)
    def _():
        greet_slab(s + 1)

    @pl.when(is_second)
    def _():
        greet_slab(s - 1)

    @pl.when(meets_late)
    def _():
        greet(0)

    up = pltpu.make_async_remote_copy(
        src_ref=own,
        dst_ref=window.at[0:4],
        send_sem=halo_send.at[0],
        recv_sem=halo_recv.at[0],
        device_id={"slab": jnp.minimum(s + 1, slabs - 1)},
        device_id_type=MESH,
    )
    down = pltpu.make_async_remote_copy(
        src_ref=own,
        dst_ref=window.at[8:12],
        send_sem=halo_send.at[1],
        recv_sem=halo_recv.at[1],
        device_id={"slab": jnp.maximum(s - 1, 0)},
        device_id_type=MESH,
    )

    @pl.when(upper & jnp.logical_not(upper_second))
    def _():
        up.start()

    @pl.when(s > 0)
    def _():
        down.start()

    y = (g // 2) % 8
    mine = pl.ds(pl.multiple_of(y * 128 + (g // 16) * 32 + (g % 2) * 16, 16), 16)

    def rows_copy(other):
        return pltpu.make_async_remote_copy(
            src_ref=outgoing.at[pl.ds(pl.multiple_of(16 * other, 16), 16)],
            dst_ref=received.at[mine],
            send_sem=rows_send,
            recv_sem=rows_recv.at[jnp.where(late, 4, y // 2)],
            device_id={"grp": other},
            device_id_type=MESH,
        )

    each(lambda other: rows_copy(other).start(), True)
    each(lambda other: rows_copy(other).start(), False)

    received[mine, :] = outgoing[pl.ds(pl.multiple_of(16 * g, 16), 16), :]

    loads[4].wait()
    near_index(near, tile, spot)
    near_hot(spot, hots)
    loads[5].wait()
    operator_parts(ops, pad, first, second)
    loads[6].wait()
    loads[7].wait()
    source = entry_source[...]
    place = ((source >> 5) & 7) * 128 + (source >> 8) * 32 + (source & 31)
    index_row[...] = entry_kind[...] * 1024 + place
    index_load = pltpu.make_async_copy(index_row, index, load_sem.at[9])
    index_load.start()
    loads[8].wait()
    target_table(entry_target, hot)
    near_table(window, cells, 1)

    @pl.when(upper_second)
    def _():
        pl.semaphore_wait(barrier, 1)
        up.start()

    @pl.when(s == 0)
    def _():
        window[0:4] = jnp.zeros((4, 64, 128), F32)

    @pl.when(s == slabs - 1)
    def _():
        window[8:12] = jnp.zeros((4, 64, 128), F32)

    @pl.when(s > 0)
    def _():
        up.wait_recv()

    @pl.when(s < slabs - 1)
    def _():
        down.wait_recv()

    near_table(window, cells, 0)
    near_table(window, cells, 2)
    near_gather(cells, tile, hots, sources)

    near_sum(own, sources, pot)
    near_out(pot, flip, pot_rows)
    index_load.wait()

    def arrived(count, k):
        block = pl.ds(0, 16 * count)
        return pltpu.make_async_remote_copy(
            src_ref=outgoing.at[block],
            dst_ref=received.at[block],
            send_sem=rows_send,
            recv_sem=rows_recv.at[k],
            device_id={"grp": lax.rem(g + 1, GROUPS)},
            device_id_type=MESH,
        )

    for i, turn in enumerate((2, 1, 3, 0)):
        k = lax.rem(jnp.where(s == 0, 1 + i, y // 2 + turn), 4)
        if i == 3:

            @pl.when(meets_late)
            def _():
                arrived(1, 4).wait_recv()
                rows_copy(0).start()

        missing = jnp.where(y // 2 == k, 1, 0)
        if i == 3:
            missing = missing + jnp.where(meets_late, 1, 0)
        for count in (14, 15, 16):

            @pl.when(missing == 16 - count)
            def _():
                arrived(count, k).wait_recv()

        start = pl.multiple_of(256 * k, 256)
        translate(received[pl.ds(start, 256), :], first, second, table, start)

    collect_sum(index, table, hot, even, odd, total, 1024)
    far_out(total, far_rows)

    arrived(GROUPS - 1, 0).wait_send()

    @pl.when(s < slabs - 1)
    def _():
        up.wait_send()

    @pl.when(s > 0)
    def _():
        down.wait_send()


def shards(
    coords,
    charges,
    multipoles,
    operators,
    send_list,
    near_list,
    m2l_source,
    m2l_target,
    m2l_operator,
):
    operands = (
        coords,
        charges.reshape(64, 128),
        multipoles,
        jnp.transpose(operators, (1, 0, 2)),
        send_list,
        near_list.T,
        m2l_source,
        m2l_target,
        m2l_operator,
    )
    hbm = pl.BlockSpec(memory_space=pltpu.HBM)
    vmem, dma = pltpu.VMEM, pltpu.SemaphoreType.DMA
    far, pot = pl.pallas_call(
        kernel,
        out_shape=[vmem((121, 512), F32), vmem((64, 128), F32)],
        in_specs=[hbm] * 9,
        out_specs=[pl.BlockSpec(memory_space=vmem)] * 2,
        scratch_shapes=[
            vmem((3, 8192), F32),
            vmem((64, 128), F32),
            vmem((121, 512), F32),
            vmem((121, 8, 121), F32),
            vmem((1, 1024), I32),
            vmem((8, 512), I32),
            vmem((1, 4096), I32),
            vmem((1, 4096), I32),
            vmem((1, 4096), I32),
            vmem((1, 4096), I32),
            pltpu.SMEM((1, 4096), I32),
            vmem((2, 128, 128), F32),
            vmem((12, 64, 128), F32),
            vmem((4, 8, 128), I32),
            vmem((4, 8, 128), I32),
            vmem((16, 256, 256), BF16),
            vmem((768, 256), BF16),
            vmem((4, 8, 64, 128), F32),
            vmem((4, 16, 128), F32),
            vmem((128, 128), F32),
            vmem((128, 512), F32),
            vmem((1024, 128), F32),
            vmem((1024, 128), F32),
            vmem((128, 128), F32),
            vmem((4, 256, 256), BF16),
            vmem((4, 256, 128), BF16),
            vmem((8192, 128), F32),
            vmem((512, 4096), BF16),
            vmem((1024, 128), F32),
            vmem((1024, 128), F32),
            vmem((512, 256), F32),
            dma((10,)),
            dma((2,)),
            dma((2,)),
            dma,
            dma((5,)),
        ],
        compiler_params=pltpu.CompilerParams(
            collective_id=0, has_side_effects=True, vmem_limit_bytes=48 * 2**20
        ),
    )(*(pltpu.with_memory_space_constraint(x, pltpu.HBM) for x in operands))
    return far, pot.reshape(-1)


def solution(mesh):
    both = ("slab", "grp")
    return jax.shard_map(
        shards,
        mesh=mesh,
        in_specs=(P(None, both), P(both), P(None, both), P()) + (P(both, None),) * 5,
        out_specs=(P(None, both), P(both)),
        check_vma=False,
    )
```
